32 devices in a mesh: row: 16 (over z, y, core), col: 2 (over x).
Axes of the slice: x: 2, y: 2, z: 4, core: 2. Of those that a mesh axis runs over, the one named last changes fastest.
Arguments:
- feature_map: bfloat16 [128, 64, 384], P('row', 'col'), may hold values from -6 to 6
- kernel: float32 [7, 7, 384], replicated, may hold values from -0.875 to 0.875
- ln_gain: float32 [384], replicated, may hold values from 0.5 to 1.5
- ln_bias: float32 [384], replicated, may hold values from -3 to 3
- w_in: bfloat16 [384, 1536], P(None, ('row', 'col')), may hold values from -0.3125 to 0.3125
- b_in: float32 [1536], replicated, may hold values from -3 to 3
- w_out: bfloat16 [1536, 384], P(('row', 'col')), may hold values from -0.15625 to 0.15625
- b_out: float32 [384], replicated, may hold values from -3 to 3
- layer_scale: float32 [384], replicated, may hold values from 0.5 to 1.5
- cotangent: bfloat16 [128, 64, 384], P('row', 'col'), may hold values from -6 to 6
Outputs:
- block_out: bfloat16 [128, 64, 384], P('row', 'col')
- grad_input: bfloat16 [128, 64, 384], P('row', 'col')
- grad_w_in: float32 [384, 1536], P(None, ('row', 'col'))
- grad_w_out: float32 [1536, 384], P(('row', 'col'))
- small_grads: float32 [53, 384], replicated
- grad_b_in: float32 [1536], replicated
The draws below stay inside these ranges and needn't reach their ends.
All inputs are finite; a program needn't handle non-finite values.
Results may differ from the reference program's by a relative error of at most 0.007.
Values may be sent and summed in bfloat16 or wider, within the bound.
A program may use at most 64 MiB of HBM per device.

```python
import math
import jax
import jax.numpy as jnp
from jax import lax

C = 384
HID = 1536
KS = 7
HEIGHT = 128
WIDTH = 64


def shard_levels(stream_key, extent, cuts, low, high):
    loudness, own = 1.0, jax.random.fold_in(stream_key, 6)
    for axis_at, blocks in cuts:
        draws = jnp.exp(jax.random.uniform(jax.random.fold_in(own, axis_at), (blocks,), jnp.float32, low / len(cuts), high / len(cuts)))
        loudness = loudness * jnp.repeat(draws, extent[axis_at] // blocks).reshape([-1 if axis == axis_at else 1 for axis in range(len(extent))])
    return loudness


def scatter_about(key, shape, spread, bound, pieces=(), dtype=jnp.bfloat16):
    array = spread * jax.random.normal(key, shape, jnp.float32)
    if pieces:
        array = array * shard_levels(key, shape, pieces, -0.22, 0.18)
    return jnp.clip(array, -bound, bound).astype(dtype)


def setup_inputs(seed: int = 0) -> dict:
    arg_keys = jax.random.split(jax.random.key(seed), 11)
    feature_map = scatter_about(arg_keys[0], (HEIGHT, WIDTH, C), 1.0, 6.0, ((0, 16), (1, 2)))
    kernel = scatter_about(arg_keys[1], (KS, KS, C), (KS * KS) ** -0.5, 0.875, (), jnp.float32)
    ln_gain = jnp.clip(1.0 + 0.1 * jax.random.normal(arg_keys[2], (C,), jnp.float32), 0.5, 1.5)
    ln_bias = scatter_about(arg_keys[3], (C,), 0.5, 3.0, (), jnp.float32)
    w_in = scatter_about(arg_keys[4], (C, HID), C ** -0.5, 0.3125, ((1, 32),))
    b_in = scatter_about(arg_keys[5], (HID,), 0.5, 3.0, (), jnp.float32)
    w_out = scatter_about(arg_keys[6], (HID, C), HID ** -0.5, 0.15625, ((0, 32),))
    b_out = scatter_about(arg_keys[7], (C,), 0.5, 3.0, (), jnp.float32)
    layer_scale = jnp.clip(1.0 + 0.1 * jax.random.normal(arg_keys[8], (C,), jnp.float32), 0.5, 1.5)
    cotangent = scatter_about(arg_keys[9], (HEIGHT, WIDTH, C), 1.0, 6.0, ((0, 16), (1, 2)))
    return dict(feature_map=feature_map, kernel=kernel, ln_gain=ln_gain, ln_bias=ln_bias, w_in=w_in, b_in=b_in, w_out=w_out, b_out=b_out, layer_scale=layer_scale, cotangent=cotangent)


def gelu_parts(hidden):
    normal_cdf = 0.5 * (1.0 + jax.scipy.special.erf(hidden * (1.0 / math.sqrt(2.0))))
    density = jnp.exp(-0.5 * hidden * hidden) * (1.0 / math.sqrt(2.0 * math.pi))
    return (hidden * normal_cdf, normal_cdf + hidden * density)

def depthwise(padded, kernel, height, width):
    result = jnp.zeros((height, width, padded.shape[2]), jnp.float32)
    for tap_row in range(7):
        for tap_col in range(7):
            result = result + padded[tap_row:tap_row + height, tap_col:tap_col + width] * kernel[tap_row, tap_col]
    return result

def reference(feature_map, kernel, ln_gain, ln_bias, w_in, b_in, w_out, b_out, layer_scale, cotangent):
    height, width, channels = feature_map.shape
    source = feature_map.astype(jnp.float32)
    padded = jnp.pad(source, ((3, 3), (3, 3), (0, 0)))
    conv = depthwise(padded, kernel, height, width)
    average = lax.optimization_barrier(jnp.mean(conv, -1, keepdims=True))
    centered = conv - average
    variance = lax.optimization_barrier(jnp.mean(centered * centered, -1, keepdims=True))
    inv_std = lax.rsqrt(variance + 1e-06)
    unit_scaled = centered * inv_std
    normed = (unit_scaled * ln_gain + ln_bias).astype(jnp.bfloat16)

    def row_step(carry, inputs):
        acc_win, acc_wout, acc_bin, acc_bout, acc_scale = carry
        normed_row, source_row, cot_row = inputs
        hidden = jnp.dot(normed_row, w_in, preferred_element_type=jnp.float32) + b_in
        act_value, slope = gelu_parts(hidden)
        activated = act_value.astype(jnp.bfloat16)
        mixed = jnp.dot(activated, w_out, preferred_element_type=jnp.float32) + b_out
        out_row = (source_row.astype(jnp.float32) + layer_scale * mixed).astype(jnp.bfloat16)
        grad_flow = cot_row.astype(jnp.float32)
        grad_mixed = grad_flow * layer_scale
        mixed_low = grad_mixed.astype(jnp.bfloat16)
        acc_wout = acc_wout + jnp.dot(activated.T, mixed_low, preferred_element_type=jnp.float32)
        grad_act = jnp.dot(mixed_low, w_out.T, preferred_element_type=jnp.float32)
        grad_hidden = (grad_act * slope).astype(jnp.bfloat16)
        acc_win = acc_win + jnp.dot(normed_row.T, grad_hidden, preferred_element_type=jnp.float32)
        acc_bin = acc_bin + lax.optimization_barrier(jnp.sum(grad_hidden.astype(jnp.float32), 0))
        acc_bout = acc_bout + lax.optimization_barrier(jnp.sum(grad_mixed, 0))
        acc_scale = acc_scale + lax.optimization_barrier(jnp.sum(grad_flow * mixed, 0))
        grad_normed = jnp.dot(grad_hidden, w_in.T, preferred_element_type=jnp.float32)
        return ((acc_win, acc_wout, acc_bin, acc_bout, acc_scale), (out_row, grad_normed))
    hidden_count = w_in.shape[1]
    start_carry = (jnp.zeros((channels, hidden_count), jnp.float32), jnp.zeros((hidden_count, channels), jnp.float32), jnp.zeros((hidden_count,), jnp.float32), jnp.zeros((channels,), jnp.float32), jnp.zeros((channels,), jnp.float32))
    sums, outputs = lax.scan(row_step, start_carry, (normed, feature_map, cotangent))
    grad_win, grad_wout, grad_bin, grad_bout, grad_scale = sums
    block_out, grad_normed = outputs
    grad_gain = lax.optimization_barrier(jnp.sum(grad_normed * unit_scaled, (0, 1)))
    grad_lnb = lax.optimization_barrier(jnp.sum(grad_normed, (0, 1)))
    scaled_grad = grad_normed * ln_gain
    grad_conv = inv_std * (scaled_grad - lax.optimization_barrier(jnp.mean(scaled_grad, -1, keepdims=True)) - unit_scaled * lax.optimization_barrier(jnp.mean(scaled_grad * unit_scaled, -1, keepdims=True)))
    tap_terms = []
    for tap_row in range(7):
        for tap_col in range(7):
            tap_terms.append(lax.optimization_barrier(jnp.sum(padded[tap_row:tap_row + height, tap_col:tap_col + width] * grad_conv, (0, 1))))
    grad_low = grad_conv.astype(jnp.bfloat16)
    grad_pad = jnp.pad(grad_low.astype(jnp.float32), ((3, 3), (3, 3), (0, 0)))
    back_conv = jnp.zeros((height, width, channels), jnp.float32)
    for tap_row in range(7):
        for tap_col in range(7):
            back_conv = back_conv + grad_pad[6 - tap_row:6 - tap_row + height, 6 - tap_col:6 - tap_col + width] * kernel[tap_row, tap_col]
    grad_input = (cotangent.astype(jnp.float32) + back_conv).astype(jnp.bfloat16)
    small_grads = jnp.concatenate([jnp.stack(tap_terms, 0), grad_gain[None], grad_lnb[None], grad_bout[None], grad_scale[None]], 0)
    return (block_out, grad_input, grad_win, grad_wout, small_grads, grad_bin)
```

```python
import functools
import math

import jax
import jax.numpy as jnp
from jax import lax
from jax.experimental import pallas as pl
from jax.experimental.pallas import tpu as pltpu
from jax.sharding import PartitionSpec as P


def padded_2(x, sides, width):
    for axis, dim in sides:
        peers, length = (lax.axis_size(axis), x.shape[dim])
        up = [(i, (i + 1) % peers) for i in range(peers - 1)]
        down = [(j, i) for i, j in up]
        last = lax.slice_in_dim(x, length - width, length, axis=dim)
        first = lax.slice_in_dim(x, 0, width, axis=dim)
        before = lax.ppermute(last, axis, up)
        after = lax.ppermute(first, axis, down)
        x = jnp.concatenate([before, x, after], axis=dim)
    return x


def gelu_parts(hidden):
    normal_cdf = 0.5 * (1.0 + jax.scipy.special.erf(hidden * (1.0 / math.sqrt(2.0))))
    density = jnp.exp(-0.5 * hidden * hidden) * (1.0 / math.sqrt(2.0 * math.pi))
    return (hidden * normal_cdf, normal_cdf + hidden * density)


def extend(field):
    return padded_2(field, (("row", 0), ("col", 1)), 3)


def spread_plan(
    feature_map, kernel, ln_gain, ln_bias, w_in, b_in, w_out, b_out, layer_scale, cotangent
):
    row_count, col_count, channels = feature_map.shape
    pixels = row_count * col_count
    padded = extend(feature_map).astype(jnp.float32)
    conv = jnp.zeros((row_count, col_count, channels), jnp.float32)
    for tap_row in range(7):
        for tap_col in range(7):
            conv = (
                conv
                + padded[tap_row : tap_row + row_count, tap_col : tap_col + col_count]
                * kernel[tap_row, tap_col]
            )
    average = jnp.mean(conv, -1, keepdims=True)
    centered = conv - average
    variance = jnp.mean(centered * centered, -1, keepdims=True)
    inv_std = lax.rsqrt(variance + 1e-06)
    unit_scaled = centered * inv_std
    normed = (unit_scaled * ln_gain + ln_bias).astype(jnp.bfloat16).reshape(pixels, channels)
    contract_last = (((1,), (1,)), ((), ()))
    contract_first = (((0,), (0,)), ((), ()))
    w_in_full = lax.all_gather(w_in, ("row", "col"), axis=1, tiled=True)
    w_out_full = lax.all_gather(w_out, ("row", "col"), axis=0, tiled=True)
    hidden = jnp.dot(normed, w_in_full, preferred_element_type=jnp.float32) + b_in
    act_value, slope = gelu_parts(hidden)
    activated = act_value.astype(jnp.bfloat16)
    mixed = jnp.dot(activated, w_out_full, preferred_element_type=jnp.float32) + b_out
    source = feature_map.astype(jnp.float32).reshape(pixels, channels)
    block_out = (
        (source + layer_scale * mixed).astype(jnp.bfloat16).reshape(row_count, col_count, channels)
    )
    grad_flow = cotangent.astype(jnp.float32).reshape(pixels, channels)
    grad_mixed = grad_flow * layer_scale
    mixed_low = grad_mixed.astype(jnp.bfloat16)
    grad_act = lax.dot_general(
        mixed_low, w_out_full, contract_last, preferred_element_type=jnp.float32
    )
    grad_hidden = (grad_act * slope).astype(jnp.bfloat16)
    grad_w_out = lax.psum_scatter(
        lax.dot_general(activated, mixed_low, contract_first, preferred_element_type=jnp.float32),
        ("row", "col"),
        scatter_dimension=0,
        tiled=True,
    )
    win_term = lax.dot_general(
        normed, grad_hidden, contract_first, preferred_element_type=jnp.float32
    )
    grad_w_in = lax.psum_scatter(win_term, ("row", "col"), scatter_dimension=1, tiled=True)
    grad_normed = lax.dot_general(
        grad_hidden, w_in_full, contract_last, preferred_element_type=jnp.float32
    )
    grad_normed = grad_normed.reshape(row_count, col_count, channels)
    grad_gain = jnp.sum(grad_normed * unit_scaled, (0, 1))
    grad_lnb = jnp.sum(grad_normed, (0, 1))
    scaled_grad = grad_normed * ln_gain
    grad_conv = inv_std * (
        scaled_grad
        - jnp.mean(scaled_grad, -1, keepdims=True)
        - unit_scaled * jnp.mean(scaled_grad * unit_scaled, -1, keepdims=True)
    )
    tap_terms = []
    for tap_row in range(7):
        for tap_col in range(7):
            tap_terms.append(
                jnp.sum(
                    padded[tap_row : tap_row + row_count, tap_col : tap_col + col_count]
                    * grad_conv,
                    (0, 1),
                )
            )
    grad_pad = extend(grad_conv.astype(jnp.bfloat16)).astype(jnp.float32)
    back_conv = jnp.zeros((row_count, col_count, channels), jnp.float32)
    for tap_row in range(7):
        for tap_col in range(7):
            back_conv = (
                back_conv
                + grad_pad[
                    6 - tap_row : 6 - tap_row + row_count, 6 - tap_col : 6 - tap_col + col_count
                ]
                * kernel[tap_row, tap_col]
            )
    grad_input = (cotangent.astype(jnp.float32) + back_conv).astype(jnp.bfloat16)
    small_local = jnp.concatenate(
        [
            jnp.stack(tap_terms, 0),
            grad_gain[None],
            grad_lnb[None],
            jnp.sum(grad_mixed, 0)[None],
            jnp.sum(grad_flow * mixed, 0)[None],
        ],
        0,
    )
    bias_local = jnp.sum(grad_hidden.astype(jnp.float32), 0)
    small_grads, grad_b_in = lax.psum((small_local, bias_local), ("row", "col"))
    return (block_out, grad_input, grad_w_in, grad_w_out, small_grads, grad_b_in)


MESH = pl.DeviceIdType.MESH
SIDES = [(a, b) for a in (-1, 0, 1) for b in (-1, 0, 1) if (a, b) != (0, 0)]
EDGE = 16
LANES = 128
CONTRACT_LAST = (((1,), (1,)), ((), ()))
CONTRACT_FIRST = (((0,), (0,)), ((), ()))


def bit_orders(rows, cols):
    bits = (rows * cols).bit_length() - 1
    pair = cols.bit_length() - 1
    rest = [b for b in range(bits - 1, -1, -1) if b != pair]
    orders = [rest, rest[-1:] + rest[:-1], rest[-2:] + rest[:-2]]
    return [order + [pair] for order in orders]


def fused_kernel(
    rows,
    cols,
    orders,
    x_ref,
    taps_ref,
    vec_ref,
    bin_ref,
    shard_ref,
    cot_ref,
    out_ref,
    gin_ref,
    gwin_ref,
    gwout_ref,
    small_ref,
    gbin_ref,
    xpad,
    gpad,
    wide,
    conv,
    unit,
    normed,
    mixed_low,
    mixed,
    gnorm,
    weights,
    total,
    leaving,
    arriving,
    sums,
    sums_in,
    halo_send,
    halo_recv,
    gather_send,
    gather_recv,
    scatter_send,
    scatter_recv,
    sum_send,
    sum_recv,
):
    height, width, channels = x_ref.shape
    pixels = height * width
    parts = len(orders)
    steps = len(orders[0])
    unit_rows = shard_ref.shape[2]
    chunk = weights.shape[2] * unit_rows
    row, col = lax.axis_index("row"), lax.axis_index("col")
    me = row * cols + col
    f32, bf16 = jnp.float32, jnp.bfloat16

    def bit_of(b):
        return lax.rem(lax.div(me, 2**b), 2)

    def partner(b):
        other = me + (1 - 2 * bit_of(b)) * 2**b
        return (lax.div(other, cols), lax.rem(other, cols))

    places = []
    for order in orders:
        place = 0
        for step, b in enumerate(order):
            place = place + bit_of(b) * 2**step
        places.append(place)

    def exists(side):
        dr, dc = side
        there = None
        for delta, at, count in ((dr, row, rows), (dc, col, cols)):
            if delta:
                ok = at > 0 if delta < 0 else at < count - 1
                there = ok if there is None else jnp.logical_and(there, ok)
        return there

    def halo_copy(source, pad, which, side, receiving):
        dr, dc = side
        at = SIDES.index(side)
        back = SIDES.index((-dr, -dc))
        row_from = {-1: pl.ds(0, 3), 0: pl.ds(0, height), 1: pl.ds(height - 3, 3)}[dr]
        col_from = {-1: pl.ds(0, EDGE), 0: pl.ds(0, width), 1: pl.ds(width - EDGE, EDGE)}[dc]
        into_r, into_c = (dr, dc) if receiving else (-dr, -dc)
        row_to = {-1: pl.ds(0, 3), 0: pl.ds(3, height), 1: pl.ds(height + 3, 3)}[into_r]
        col_to = {-1: pl.ds(0, EDGE), 0: pl.ds(EDGE, width), 1: pl.ds(width + EDGE, EDGE)}[into_c]
        return pltpu.make_async_remote_copy(
            src_ref=source.at[row_from, col_from],
            dst_ref=pad.at[row_to, col_to],
            send_sem=halo_send.at[which, at],
            recv_sem=halo_recv.at[which, back if receiving else at],
            device_id=(row + dr, col + dc),
            device_id_type=MESH,
        )

    def halo_start(source, pad, which):
        for side in SIDES:

            @pl.when(exists(side))
            def _():
                halo_copy(source, pad, which, side, False).start()

    def halo_wait(source, pad, which):
        for side in SIDES:

            @pl.when(exists(side))
            def _():
                halo_copy(source, pad, which, side, False).wait_send()
                halo_copy(source, pad, which, side, True).wait_recv()

    def gather_copy(part, step):
        size = 2**step
        held = weights.at[part, :, pl.ds(lax.div(places[part], size) * size, size)]
        return pltpu.make_async_remote_copy(
            src_ref=held,
            dst_ref=held,
            send_sem=gather_send.at[part, step],
            recv_sem=gather_recv.at[part, step],
            device_id=partner(orders[part][step]),
            device_id_type=MESH,
        )

    def gather_turn(part, step):
        if step:
            gather_copy(part, step - 1).wait()
        if step < steps:
            gather_copy(part, step).start()

    def scatter_copy(part, step):
        size = 2**step
        return pltpu.make_async_remote_copy(
            src_ref=leaving.at[part, :, pl.ds(size, size)],
            dst_ref=arriving.at[part, :, pl.ds(size, size)],
            send_sem=scatter_send.at[part, step],
            recv_sem=scatter_recv.at[part, step],
            device_id=partner(orders[part][step]),
            device_id_type=MESH,
        )

    def scatter_start(part, step):
        size = 2**step
        mine = lax.div(places[part], size)
        away = (mine + 1 - 2 * lax.rem(mine, 2)) * size
        leaving[part, :, size : 2 * size] = total[part, :, pl.ds(away, size)].astype(bf16)
        scatter_copy(part, step).start()

    def scatter_turn(part, step):
        size = 2**step
        scatter_copy(part, step).wait()
        keep = pl.ds(lax.div(places[part], size) * size, size)
        total[part, :, keep] = total[part, :, keep] + arriving[part, :, size : 2 * size].astype(f32)
        if step:
            scatter_start(part, step - 1)

    def scatter_turns(step):
        for part in range(parts):
            scatter_turn(part, step)

    def sum_copy(step):
        return pltpu.make_async_remote_copy(
            src_ref=sums.at[step],
            dst_ref=sums_in.at[step],
            send_sem=sum_send.at[step],
            recv_sem=sum_recv.at[step],
            device_id=partner(orders[0][steps - 1 - step]),
            device_id_type=MESH,
        )

    def sum_turn(step):
        sum_copy(step).wait()
        sums[step + 1] = sums[step] + sums_in[step]
        if step + 1 < steps:
            sum_copy(step + 1).start()

    gain, offset = vec_ref[0:1, :], vec_ref[1:2, :]
    out_bias, scale = vec_ref[2:3, :], vec_ref[3:4, :]

    xpad[...] = jnp.zeros_like(xpad)
    gpad[...] = jnp.zeros_like(gpad)
    for part in range(parts):
        weights[part, :, pl.ds(places[part], 1)] = shard_ref[part][:, None]

    barrier = pltpu.get_barrier_semaphore()
    expected = steps
    for b in range(steps):
        pl.semaphore_signal(barrier, inc=1, device_id=partner(b), device_id_type=MESH)
    for side in SIDES:
        here = exists(side)
        expected = expected + jnp.where(here, 1, 0)

        @pl.when(here)
        def _():
            pl.semaphore_signal(
                barrier, inc=1, device_id=(row + side[0], col + side[1]), device_id_type=MESH
            )

    pl.semaphore_wait(barrier, expected)

    halo_start(x_ref, xpad, 0)
    for part in range(parts):
        gather_turn(part, 0)

    xpad[3 : 3 + height, EDGE : EDGE + width] = x_ref[...]
    sums[0, 48:64] = jnp.zeros((16, channels), f32)
    grad_mixed = cot_ref[...].astype(f32).reshape(pixels, channels) * scale
    mixed_low[...] = grad_mixed.astype(bf16)
    sums[0, 51:52] = jnp.sum(grad_mixed, 0, keepdims=True)

    halo_wait(x_ref, xpad, 0)
    for part in range(parts):
        gather_turn(part, 1)
    wide[...] = xpad[:, 8 : width + 24].astype(f32)

    def window(shift, lanes):
        return wide[:, 5 + shift : 5 + shift + width, lanes]

    def stencil(lanes, flip):
        result = jnp.zeros((height, width, LANES), f32)
        for tap_col in range(7):
            shifted = window(tap_col, lanes)
            for tap_row in range(7):
                at = tap_row * 7 + tap_col
                at = 48 - at if flip else at
                result = result + shifted[tap_row : tap_row + height] * taps_ref[at : at + 1, lanes]
        return result

    blocks = channels // LANES
    for block in range(blocks):
        lanes = slice(block * LANES, (block + 1) * LANES)
        conv[:, lanes] = stencil(lanes, False).reshape(pixels, LANES)
        if block + 2 < steps:
            for part in range(parts):
                gather_turn(part, block + 2)

    centered = conv[...]
    centered = centered - jnp.mean(centered, -1, keepdims=True)
    inv_std = lax.rsqrt(jnp.mean(centered * centered, -1, keepdims=True) + 1e-06)
    unit[...] = centered * inv_std
    normed[...] = (unit[...] * gain + offset).astype(bf16)
    for step in range(blocks + 2, steps + 1):
        for part in range(parts):
            gather_turn(part, step)

    for part in range(parts):
        win = weights[part, 0].reshape(chunk, channels)
        wout = weights[part, 1].reshape(chunk, channels)
        hidden = (
            lax.dot_general(normed[...], win, CONTRACT_LAST, preferred_element_type=f32)
            + bin_ref[part : part + 1, :]
        )
        act_value, slope = gelu_parts(hidden)
        activated = act_value.astype(bf16)
        grad_act = lax.dot_general(
            mixed_low[...], wout, CONTRACT_LAST, preferred_element_type=f32
        )
        grad_hidden = (grad_act * slope).astype(bf16)
        total[part, 1] = lax.dot_general(
            activated, mixed_low[...], CONTRACT_FIRST, preferred_element_type=f32
        ).reshape(-1, unit_rows, channels)
        total[part, 0] = lax.dot_general(
            grad_hidden, normed[...], CONTRACT_FIRST, preferred_element_type=f32
        ).reshape(-1, unit_rows, channels)
        scatter_start(part, steps - 1)
        mixed_term = jnp.dot(activated, wout, preferred_element_type=f32)
        gnorm_term = jnp.dot(grad_hidden, win, preferred_element_type=f32)
        mixed[...] = mixed_term if part == 0 else mixed[...] + mixed_term
        gnorm[...] = gnorm_term if part == 0 else gnorm[...] + gnorm_term
        bias_sum = jnp.sum(grad_hidden.astype(f32), 0, keepdims=True)
        for piece in range(chunk // LANES):
            at = part * (chunk // LANES) + piece
            sums[0, 53 + at // blocks : 54 + at // blocks, at % blocks * LANES : (at % blocks + 1) * LANES] = (
                bias_sum[:, piece * LANES : (piece + 1) * LANES]
            )

    scatter_turns(steps - 1)
    grad_normed = gnorm[...]
    unit_scaled = unit[...]
    sums[0, 49:50] = jnp.sum(grad_normed * unit_scaled, 0, keepdims=True)
    sums[0, 50:51] = jnp.sum(grad_normed, 0, keepdims=True)
    scaled = grad_normed * gain
    grad_conv = inv_std * (
        scaled
        - jnp.mean(scaled, -1, keepdims=True)
        - unit_scaled * jnp.mean(scaled * unit_scaled, -1, keepdims=True)
    )
    conv[...] = grad_conv
    normed[...] = grad_conv.astype(bf16)
    gpad[3 : 3 + height, EDGE : EDGE + width] = normed[...].reshape(height, width, channels)
    grad_block = gpad.at[pl.ds(3, height), pl.ds(EDGE, width)]
    halo_start(grad_block, gpad, 1)

    mixed_full = mixed[...] + out_bias
    source = x_ref[...].astype(f32).reshape(pixels, channels)
    out_ref[...] = (source + scale * mixed_full).astype(bf16).reshape(height, width, channels)
    grad_flow = cot_ref[...].astype(f32).reshape(pixels, channels)
    sums[0, 52:53] = jnp.sum(grad_flow * mixed_full, 0, keepdims=True)

    for block in range(blocks):
        lanes = slice(block * LANES, (block + 1) * LANES)
        grad_part = conv[:, lanes].reshape(height, width, LANES)
        for tap_col in range(7):
            shifted = window(tap_col, lanes)
            for tap_row in range(7):
                at = tap_row * 7 + tap_col
                term = shifted[tap_row : tap_row + height] * grad_part
                sums[0, at : at + 1, lanes] = jnp.sum(
                    term.reshape(pixels, LANES), 0, keepdims=True
                )
        if block == 0:
            scatter_turns(steps - 2)
    sum_copy(0).start()
    scatter_turns(steps - 3)

    halo_wait(grad_block, gpad, 1)
    wide[...] = gpad[:, 8 : width + 24].astype(f32)
    for block in range(blocks):
        lanes = slice(block * LANES, (block + 1) * LANES)
        gin_ref[:, :, lanes] = (
            cot_ref[:, :, lanes].astype(f32) + stencil(lanes, True)
        ).astype(bf16)
        sum_turn(block)
        if steps - 4 - block >= 0:
            scatter_turns(steps - 4 - block)
    for step in range(steps - 4 - blocks, -1, -1):
        scatter_turns(step)
    for step in range(blocks, steps):
        sum_turn(step)
    for part in range(parts):
        at = slice(part * unit_rows, (part + 1) * unit_rows)
        own = total[part, :, pl.ds(places[part], 1)]
        gwin_ref[at, :] = own[0, 0]
        gwout_ref[at, :] = own[1, 0]
    small_ref[...] = sums[steps, 0:53]
    gbin_ref[...] = sums[steps, 53:57]


def on_device(
    rows,
    cols,
    feature_map,
    kernel,
    ln_gain,
    ln_bias,
    w_in,
    b_in,
    w_out,
    b_out,
    layer_scale,
    cotangent,
):
    devices = rows * cols
    parts = 3
    height, width, channels = feature_map.shape
    units = w_out.shape[0]
    steps = devices.bit_length() - 1
    if units % (16 * parts) or devices != 2**steps or steps < 5 or devices * units != 4 * channels:
        return spread_plan(
            feature_map, kernel, ln_gain, ln_bias, w_in, b_in, w_out, b_out, layer_scale, cotangent
        )
    orders = bit_orders(rows, cols)
    piece = units // parts
    pixels = height * width
    shard = jnp.stack([w_in.T, w_out]).reshape(2, parts, piece, channels).transpose(1, 0, 2, 3)
    vectors = jnp.stack([ln_gain, ln_bias, b_out, layer_scale])
    spread = b_in.reshape((2,) * steps + (parts, piece))
    bias = jnp.stack(
        [
            spread[..., part, :].transpose([steps - 1 - b for b in order[::-1]] + [steps]).reshape(-1)
            for part, order in enumerate(orders)
        ]
    )
    f32, bf16 = jnp.float32, jnp.bfloat16
    padded_shape = (height + 6, width + 2 * EDGE, channels)
    outs = pl.pallas_call(
        functools.partial(fused_kernel, rows, cols, orders),
        out_shape=(
            jax.ShapeDtypeStruct(feature_map.shape, bf16),
            jax.ShapeDtypeStruct(feature_map.shape, bf16),
            jax.ShapeDtypeStruct((units, channels), f32),
            jax.ShapeDtypeStruct((units, channels), f32),
            jax.ShapeDtypeStruct((53, channels), f32),
            jax.ShapeDtypeStruct((4, channels), f32),
        ),
        in_specs=[pl.BlockSpec(memory_space=pltpu.VMEM)] * 6,
        out_specs=(pl.BlockSpec(memory_space=pltpu.VMEM),) * 6,
        scratch_shapes=[
            pltpu.VMEM(padded_shape, bf16),
            pltpu.VMEM(padded_shape, bf16),
            pltpu.VMEM((height + 6, width + 16, channels), f32),
            pltpu.VMEM((pixels, channels), f32),
            pltpu.VMEM((pixels, channels), f32),
            pltpu.VMEM((pixels, channels), bf16),
            pltpu.VMEM((pixels, channels), bf16),
            pltpu.VMEM((pixels, channels), f32),
            pltpu.VMEM((pixels, channels), f32),
            pltpu.VMEM((parts, 2, devices, piece, channels), bf16),
            pltpu.VMEM((parts, 2, devices, piece, channels), f32),
            pltpu.VMEM((parts, 2, devices, piece, channels), bf16),
            pltpu.VMEM((parts, 2, devices, piece, channels), bf16),
            pltpu.VMEM((steps + 1, 64, channels), f32),
            pltpu.VMEM((steps, 64, channels), f32),
            pltpu.SemaphoreType.DMA((2, len(SIDES))),
            pltpu.SemaphoreType.DMA((2, len(SIDES))),
            pltpu.SemaphoreType.DMA((parts, steps)),
            pltpu.SemaphoreType.DMA((parts, steps)),
            pltpu.SemaphoreType.DMA((parts, steps)),
            pltpu.SemaphoreType.DMA((parts, steps)),
            pltpu.SemaphoreType.DMA((steps,)),
            pltpu.SemaphoreType.DMA((steps,)),
        ],
        compiler_params=pltpu.CompilerParams(
            collective_id=0, has_side_effects=True, vmem_limit_bytes=50 * 2**20
        ),
        name="convnext_block",
    )(feature_map, kernel.reshape(49, channels), vectors, bias, shard, cotangent)
    block_out, grad_input, grad_win, grad_wout, small_grads, bias_sums = outs
    pieces = bias_sums.reshape((parts,) + (2,) * steps + (piece,))
    ordered = []
    for part, order in enumerate(orders):
        back = [steps - 1 - order.index(b) for b in range(steps - 1, -1, -1)]
        ordered.append(pieces[part].transpose(back + [steps]).reshape(devices, piece))
    grad_b_in = jnp.stack(ordered, 1).reshape(-1)
    return (block_out, grad_input, grad_win.T, grad_wout, small_grads, grad_b_in)


def solution(mesh):
    placed = (
        P("row", "col", None),
        P(),
        P(),
        P(),
        P(None, ("row", "col")),
        P(),
        P(("row", "col"), None),
        P(),
        P(),
        P("row", "col", None),
    )
    return jax.shard_map(
        functools.partial(on_device, mesh.shape["row"], mesh.shape["col"]),
        mesh=mesh,
        in_specs=placed,
        out_specs=(
            P("row", "col", None),
            P("row", "col", None),
            P(None, ("row", "col")),
            P(("row", "col"), None),
            P(),
            P(),
        ),
        check_vma=False,
    )
```

```python
import functools
import math

import jax
import jax.numpy as jnp
from jax import lax
from jax.experimental import pallas as pl
from jax.experimental.pallas import tpu as pltpu
from jax.sharding import PartitionSpec as P


def padded_2(x, sides, width):
    for axis, dim in sides:
        peers, length = (lax.axis_size(axis), x.shape[dim])
        up = [(i, (i + 1) % peers) for i in range(peers - 1)]
        down = [(j, i) for i, j in up]
        last = lax.slice_in_dim(x, length - width, length, axis=dim)
        first = lax.slice_in_dim(x, 0, width, axis=dim)
        before = lax.ppermute(last, axis, up)
        after = lax.ppermute(first, axis, down)
        x = jnp.concatenate([before, x, after], axis=dim)
    return x


def gelu_parts(hidden):
    normal_cdf = 0.5 * (1.0 + jax.scipy.special.erf(hidden * (1.0 / math.sqrt(2.0))))
    density = jnp.exp(-0.5 * hidden * hidden) * (1.0 / math.sqrt(2.0 * math.pi))
    return (hidden * normal_cdf, normal_cdf + hidden * density)


def extend(field):
    return padded_2(field, (("row", 0), ("col", 1)), 3)


def spread_plan(
    feature_map, kernel, ln_gain, ln_bias, w_in, b_in, w_out, b_out, layer_scale, cotangent
):
    row_count, col_count, channels = feature_map.shape
    pixels = row_count * col_count
    padded = extend(feature_map).astype(jnp.float32)
    conv = jnp.zeros((row_count, col_count, channels), jnp.float32)
    for tap_row in range(7):
        for tap_col in range(7):
            conv = (
                conv
                + padded[tap_row : tap_row + row_count, tap_col : tap_col + col_count]
                * kernel[tap_row, tap_col]
            )
    average = jnp.mean(conv, -1, keepdims=True)
    centered = conv - average
    variance = jnp.mean(centered * centered, -1, keepdims=True)
    inv_std = lax.rsqrt(variance + 1e-06)
    unit_scaled = centered * inv_std
    normed = (unit_scaled * ln_gain + ln_bias).astype(jnp.bfloat16).reshape(pixels, channels)
    contract_last = (((1,), (1,)), ((), ()))
    contract_first = (((0,), (0,)), ((), ()))
    w_in_full = lax.all_gather(w_in, ("row", "col"), axis=1, tiled=True)
    w_out_full = lax.all_gather(w_out, ("row", "col"), axis=0, tiled=True)
    hidden = jnp.dot(normed, w_in_full, preferred_element_type=jnp.float32) + b_in
    act_value, slope = gelu_parts(hidden)
    activated = act_value.astype(jnp.bfloat16)
    mixed = jnp.dot(activated, w_out_full, preferred_element_type=jnp.float32) + b_out
    source = feature_map.astype(jnp.float32).reshape(pixels, channels)
    block_out = (
        (source + layer_scale * mixed).astype(jnp.bfloat16).reshape(row_count, col_count, channels)
    )
    grad_flow = cotangent.astype(jnp.float32).reshape(pixels, channels)
    grad_mixed = grad_flow * layer_scale
    mixed_low = grad_mixed.astype(jnp.bfloat16)
    grad_act = lax.dot_general(
        mixed_low, w_out_full, contract_last, preferred_element_type=jnp.float32
    )
    grad_hidden = (grad_act * slope).astype(jnp.bfloat16)
    grad_w_out = lax.psum_scatter(
        lax.dot_general(activated, mixed_low, contract_first, preferred_element_type=jnp.float32),
        ("row", "col"),
        scatter_dimension=0,
        tiled=True,
    )
    win_term = lax.dot_general(
        normed, grad_hidden, contract_first, preferred_element_type=jnp.float32
    )
    grad_w_in = lax.psum_scatter(win_term, ("row", "col"), scatter_dimension=1, tiled=True)
    grad_normed = lax.dot_general(
        grad_hidden, w_in_full, contract_last, preferred_element_type=jnp.float32
    )
    grad_normed = grad_normed.reshape(row_count, col_count, channels)
    grad_gain = jnp.sum(grad_normed * unit_scaled, (0, 1))
    grad_lnb = jnp.sum(grad_normed, (0, 1))
    scaled_grad = grad_normed * ln_gain
    grad_conv = inv_std * (
        scaled_grad
        - jnp.mean(scaled_grad, -1, keepdims=True)
        - unit_scaled * jnp.mean(scaled_grad * unit_scaled, -1, keepdims=True)
    )
    tap_terms = []
    for tap_row in range(7):
        for tap_col in range(7):
            tap_terms.append(
                jnp.sum(
                    padded[tap_row : tap_row + row_count, tap_col : tap_col + col_count]
                    * grad_conv,
                    (0, 1),
                )
            )
    grad_pad = extend(grad_conv.astype(jnp.bfloat16)).astype(jnp.float32)
    back_conv = jnp.zeros((row_count, col_count, channels), jnp.float32)
    for tap_row in range(7):
        for tap_col in range(7):
            back_conv = (
                back_conv
                + grad_pad[
                    6 - tap_row : 6 - tap_row + row_count, 6 - tap_col : 6 - tap_col + col_count
                ]
                * kernel[tap_row, tap_col]
            )
    grad_input = (cotangent.astype(jnp.float32) + back_conv).astype(jnp.bfloat16)
    small_local = jnp.concatenate(
        [
            jnp.stack(tap_terms, 0),
            grad_gain[None],
            grad_lnb[None],
            jnp.sum(grad_mixed, 0)[None],
            jnp.sum(grad_flow * mixed, 0)[None],
        ],
        0,
    )
    bias_local = jnp.sum(grad_hidden.astype(jnp.float32), 0)
    small_grads, grad_b_in = lax.psum((small_local, bias_local), ("row", "col"))
    return (block_out, grad_input, grad_w_in, grad_w_out, small_grads, grad_b_in)


MESH = pl.DeviceIdType.MESH
SIDES = [(a, b) for a in (-1, 0, 1) for b in (-1, 0, 1) if (a, b) != (0, 0)]
EDGE = 16
LANES = 128
CONTRACT_LAST = (((1,), (1,)), ((), ()))
CONTRACT_FIRST = (((0,), (0,)), ((), ()))


def bit_orders(rows, cols):
    bits = (rows * cols).bit_length() - 1
    pair = cols.bit_length() - 1
    rest = [b for b in range(bits - 1, -1, -1) if b != pair]
    orders = [rest, rest[-1:] + rest[:-1], rest[-2:] + rest[:-2]]
    return [order + [pair] for order in orders]


def fused_kernel(
    rows,
    cols,
    orders,
    x_hbm,
    taps_hbm,
    gain_hbm,
    offset_hbm,
    win_hbm,
    bin_hbm,
    wout_hbm,
    bout_hbm,
    scale_hbm,
    cot_hbm,
    out_ref,
    gin_ref,
    gwin_ref,
    gwout_ref,
    small_ref,
    gbin_ref,
    cot_ref,
    taps_ref,
    gain_ref,
    offset_ref,
    bin_ref,
    bout_ref,
    scale_ref,
    xpad,
    gpad,
    wide,
    conv,
    unit,
    normed,
    mixed_low,
    mixed,
    gnorm,
    weights,
    total,
    leaving,
    arriving,
    sums,
    sums_first,
    sums_run,
    sums_in,
    sums_all,
    local_sem,
    halo_send,
    halo_recv,
    gather_send,
    gather_recv,
    scatter_send,
    scatter_recv,
    sum_send,
    sum_recv,
):
    height, width, channels = cot_ref.shape
    pixels = height * width
    parts = len(orders)
    steps = len(orders[0])
    unit_rows = weights.shape[3]
    chunk = weights.shape[2] * unit_rows
    row, col = lax.axis_index("row"), lax.axis_index("col")
    me = row * cols + col
    f32, bf16 = jnp.float32, jnp.bfloat16

    def bit_of(b):
        return lax.rem(lax.div(me, 2**b), 2)

    def partner(b):
        other = me + (1 - 2 * bit_of(b)) * 2**b
        return (lax.div(other, cols), lax.rem(other, cols))

    places = []
    for order in orders:
        place = 0
        for step, b in enumerate(order):
            place = place + bit_of(b) * 2**step
        places.append(place)

    def exists(side):
        dr, dc = side
        there = None
        for delta, at, count in ((dr, row, rows), (dc, col, cols)):
            if delta:
                ok = at > 0 if delta < 0 else at < count - 1
                there = ok if there is None else jnp.logical_and(there, ok)
        return there

    def halo_copy(source, pad, which, side, receiving):
        dr, dc = side
        at = SIDES.index(side)
        back = SIDES.index((-dr, -dc))
        row_from = {-1: pl.ds(0, 3), 0: pl.ds(0, height), 1: pl.ds(height - 3, 3)}[dr]
        col_from = {-1: pl.ds(0, EDGE), 0: pl.ds(0, width), 1: pl.ds(width - EDGE, EDGE)}[dc]
        into_r, into_c = (dr, dc) if receiving else (-dr, -dc)
        row_to = {-1: pl.ds(0, 3), 0: pl.ds(3, height), 1: pl.ds(height + 3, 3)}[into_r]
        col_to = {-1: pl.ds(0, EDGE), 0: pl.ds(EDGE, width), 1: pl.ds(width + EDGE, EDGE)}[into_c]
        return pltpu.make_async_remote_copy(
            src_ref=source.at[row_from, col_from],
            dst_ref=pad.at[row_to, col_to],
            send_sem=halo_send.at[which, at],
            recv_sem=halo_recv.at[which, back if receiving else at],
            device_id=(row + dr, col + dc),
            device_id_type=MESH,
        )

    def halo_start(source, pad, which):
        for side in SIDES:

            @pl.when(exists(side))
            def _():
                halo_copy(source, pad, which, side, False).start()

    def halo_wait(source, pad, which):
        for side in SIDES:

            @pl.when(exists(side))
            def _():
                halo_copy(source, pad, which, side, False).wait_send()
                halo_copy(source, pad, which, side, True).wait_recv()

    def gather_copy(part, step):
        size = 2**step
        held = weights.at[part, :, pl.ds(lax.div(places[part], size) * size, size)]
        return pltpu.make_async_remote_copy(
            src_ref=held,
            dst_ref=held,
            send_sem=gather_send.at[part, step],
            recv_sem=gather_recv.at[part, step],
            device_id=partner(orders[part][step]),
            device_id_type=MESH,
        )

    def gather_turn(part, step):
        if step:
            gather_copy(part, step - 1).wait()
        if step < steps:
            gather_copy(part, step).start()

    def scatter_copy(part, step):
        size = 2**step
        return pltpu.make_async_remote_copy(
            src_ref=leaving.at[part, :, pl.ds(size, size)],
            dst_ref=arriving.at[part, :, pl.ds(size, size)],
            send_sem=scatter_send.at[part, step],
            recv_sem=scatter_recv.at[part, step],
            device_id=partner(orders[part][step]),
            device_id_type=MESH,
        )

    def scatter_start(part, step):
        size = 2**step
        mine = lax.div(places[part], size)
        away = (mine + 1 - 2 * lax.rem(mine, 2)) * size
        leaving[part, :, size : 2 * size] = total[part, :, pl.ds(away, size)].astype(bf16)
        scatter_copy(part, step).start()

    def scatter_turn(part, step):
        size = 2**step
        scatter_copy(part, step).wait()
        keep = pl.ds(lax.div(places[part], size) * size, size)
        total[part, :, keep] = total[part, :, keep] + arriving[part, :, size : 2 * size].astype(f32)
        if step:
            scatter_start(part, step - 1)

    pair_bit = orders[0][-1]
    pair_half = bit_of(pair_bit)
    sum_orders = [orders[0][:-1], orders[0][:-1][::-1]]

    def pair_copy():
        return pltpu.make_async_remote_copy(
            src_ref=sums.at[pl.ds((1 - pair_half) * 2, 2)],
            dst_ref=sums_first,
            send_sem=sum_send.at[0],
            recv_sem=sum_recv.at[0],
            device_id=partner(pair_bit),
            device_id_type=MESH,
        )

    def run_copy(step, half):
        return pltpu.make_async_remote_copy(
            src_ref=sums_run.at[step, half],
            dst_ref=sums_in.at[step, half],
            send_sem=sum_send.at[1 + 2 * step + half],
            recv_sem=sum_recv.at[1 + 2 * step + half],
            device_id=partner(sum_orders[half][step]),
            device_id_type=MESH,
        )

    def share_copy():
        own = sums_all.at[pl.ds(pair_half * 2, 2)]
        return pltpu.make_async_remote_copy(
            src_ref=own,
            dst_ref=own,
            send_sem=sum_send.at[2 * steps - 1],
            recv_sem=sum_recv.at[2 * steps - 1],
            device_id=partner(pair_bit),
            device_id_type=MESH,
        )

    def sum_turn(step):
        last = steps - 1
        if step == 0:
            pair_copy().wait()
            sums_run[0] = sums[pl.ds(pair_half * 2, 2)] + sums_first[...]
        else:
            for half in range(2):
                run_copy(step - 1, half).wait()
                added = sums_run[step - 1, half] + sums_in[step - 1, half]
                if step < last:
                    sums_run[step, half] = added
                    run_copy(step, half).start()
                else:
                    sums_all[pl.ds(pair_half * 2 + half, 1)] = added[None]
            if step == last:
                share_copy().start()
            return
        for half in range(2):
            run_copy(0, half).start()

    def put_sum(at, lanes, value):
        sums[at // 16, at % 16 : at % 16 + 1, lanes] = value

    every = slice(0, channels)
    xpad[...] = jnp.zeros_like(xpad)
    center = xpad.at[pl.ds(3, height), pl.ds(EDGE, width)]
    moves = []
    for part in range(parts):
        for which, source in enumerate((win_hbm, wout_hbm)):
            moves.append(
                (source.at[pl.ds(part * unit_rows, unit_rows)], weights.at[part, which, places[part]])
            )
    moves += [
        (x_hbm, center),
        (cot_hbm, cot_ref),
        (scale_hbm, scale_ref),
        (taps_hbm, taps_ref),
        (bin_hbm, bin_ref),
        (gain_hbm, gain_ref),
        (offset_hbm, offset_ref),
        (bout_hbm, bout_ref),
    ]
    moves = [
        pltpu.make_async_copy(source, target, local_sem.at[at])
        for at, (source, target) in enumerate(moves)
    ]
    for move in moves:
        move.start()
    gpad[...] = jnp.zeros_like(gpad)

    barrier = pltpu.get_barrier_semaphore()
    expected = steps
    for b in range(steps):
        pl.semaphore_signal(barrier, inc=1, device_id=partner(b), device_id_type=MESH)
    for side in SIDES:
        here = exists(side)
        expected = expected + jnp.where(here, 1, 0)

        @pl.when(here)
        def _():
            pl.semaphore_signal(
                barrier, inc=1, device_id=(row + side[0], col + side[1]), device_id_type=MESH
            )

    pl.semaphore_wait(barrier, expected)

    halo_start(x_hbm, xpad, 0)
    for move in moves[: 2 * parts]:
        move.wait()
    for part in range(parts):
        gather_turn(part, 0)
    for move in moves[2 * parts :]:
        move.wait()

    def as_row(ref):
        return ref[...].reshape(1, ref.shape[0])

    gain, offset = as_row(gain_ref), as_row(offset_ref)
    out_bias, scale = as_row(bout_ref), as_row(scale_ref)
    sums[3] = jnp.zeros((16, channels), f32)
    grad_mixed = cot_ref[...].astype(f32).reshape(pixels, channels) * scale
    mixed_low[...] = grad_mixed.astype(bf16)
    put_sum(51, every, jnp.sum(grad_mixed, 0, keepdims=True))

    owners = []
    for order in orders:
        owners.append(
            [
                sum(((place >> step) & 1) << b for step, b in enumerate(order))
                for place in range(2**steps)
            ]
        )
    bias_all = as_row(bin_ref)
    biases = []
    for part in range(parts):
        starts = [(owner * parts + part) * unit_rows for owner in owners[part]]
        biases.append(
            jnp.concatenate([bias_all[:, at : at + unit_rows] for at in starts], 1)
        )

    halo_wait(x_hbm, xpad, 0)
    for part in range(parts):
        gather_turn(part, 1)
    wide[...] = xpad[:, 8 : width + 24].astype(f32)

    def window(shift, lanes):
        return wide[:, 5 + shift : 5 + shift + width, lanes]

    def stencil(lanes, flip):
        result = jnp.zeros((height, width, LANES), f32)
        for tap_col in range(7):
            shifted = window(tap_col, lanes)
            for tap_row in range(7):
                a, b = (6 - tap_row, 6 - tap_col) if flip else (tap_row, tap_col)
                result = result + shifted[tap_row : tap_row + height] * taps_ref[a, b : b + 1, lanes]
        return result

    blocks = channels // LANES
    for block in range(blocks):
        lanes = slice(block * LANES, (block + 1) * LANES)
        conv[:, lanes] = stencil(lanes, False).reshape(pixels, LANES)
        if block + 2 < steps:
            for part in range(parts):
                gather_turn(part, block + 2)

    centered = conv[...]
    centered = centered - jnp.mean(centered, -1, keepdims=True)
    inv_std = lax.rsqrt(jnp.mean(centered * centered, -1, keepdims=True) + 1e-06)
    unit[...] = centered * inv_std
    normed[...] = (unit[...] * gain + offset).astype(bf16)
    for step in range(blocks + 2, steps):
        for part in range(parts):
            gather_turn(part, step)

    bias_sums = []
    for part in range(parts):
        gather_turn(part, steps)
        win = weights[part, 0].reshape(chunk, channels)
        wout = weights[part, 1].reshape(chunk, channels)
        hidden = (
            lax.dot_general(normed[...], win, CONTRACT_LAST, preferred_element_type=f32)
            + biases[part]
        )
        act_value, slope = gelu_parts(hidden)
        activated = act_value.astype(bf16)
        grad_act = lax.dot_general(
            mixed_low[...], wout, CONTRACT_LAST, preferred_element_type=f32
        )
        grad_hidden = (grad_act * slope).astype(bf16)
        total[part, 1] = lax.dot_general(
            activated, mixed_low[...], CONTRACT_FIRST, preferred_element_type=f32
        ).reshape(-1, unit_rows, channels)
        total[part, 0] = lax.dot_general(
            grad_hidden, normed[...], CONTRACT_FIRST, preferred_element_type=f32
        ).reshape(-1, unit_rows, channels)
        scatter_start(part, steps - 1)
        mixed_term = jnp.dot(activated, wout, preferred_element_type=f32)
        gnorm_term = jnp.dot(grad_hidden, win, preferred_element_type=f32)
        mixed[...] = mixed_term if part == 0 else mixed[...] + mixed_term
        gnorm[...] = gnorm_term if part == 0 else gnorm[...] + gnorm_term
        bias_sums.append(jnp.sum(grad_hidden.astype(f32), 0, keepdims=True))
        for earlier in range(part):
            scatter_turn(earlier, steps - part + earlier)

    grad_normed = gnorm[...]
    unit_scaled = unit[...]
    put_sum(49, every, jnp.sum(grad_normed * unit_scaled, 0, keepdims=True))
    put_sum(50, every, jnp.sum(grad_normed, 0, keepdims=True))
    scaled = grad_normed * gain
    grad_conv = inv_std * (
        scaled
        - jnp.mean(scaled, -1, keepdims=True)
        - unit_scaled * jnp.mean(scaled * unit_scaled, -1, keepdims=True)
    )
    conv[...] = grad_conv
    normed[...] = grad_conv.astype(bf16)
    gpad[3 : 3 + height, EDGE : EDGE + width] = normed[...].reshape(height, width, channels)
    grad_block = gpad.at[pl.ds(3, height), pl.ds(EDGE, width)]
    halo_start(grad_block, gpad, 1)
    scatter_turn(2, steps - 1)

    mixed_full = mixed[...] + out_bias
    source = center[...].astype(f32).reshape(pixels, channels)
    out_ref[...] = (source + scale * mixed_full).astype(bf16).reshape(height, width, channels)
    grad_flow = cot_ref[...].astype(f32).reshape(pixels, channels)
    put_sum(52, every, jnp.sum(grad_flow * mixed_full, 0, keepdims=True))
    for line in range(4):
        pieces = []
        for owner in range(line * 2**steps // 4, (line + 1) * 2**steps // 4):
            for part in range(parts):
                at = owners[part].index(owner) * unit_rows
                pieces.append(bias_sums[part][:, at : at + unit_rows])
        put_sum(53 + line, every, jnp.concatenate(pieces, 1))

    for block in range(blocks):
        lanes = slice(block * LANES, (block + 1) * LANES)
        grad_part = conv[:, lanes].reshape(height, width, LANES)
        for tap_col in range(7):
            shifted = window(tap_col, lanes)
            for tap_row in range(7):
                at = tap_row * 7 + tap_col
                term = shifted[tap_row : tap_row + height] * grad_part
                put_sum(at, lanes, jnp.sum(term.reshape(pixels, LANES), 0, keepdims=True))
        if block == 0:
            scatter_turn(1, steps - 2)
            scatter_turn(0, steps - 3)
    pair_copy().start()
    scatter_turn(2, steps - 2)
    scatter_turn(1, steps - 3)
    scatter_turn(0, steps - 4)

    halo_wait(grad_block, gpad, 1)
    wide[...] = gpad[:, 8 : width + 24].astype(f32)
    for block in range(blocks):
        lanes = slice(block * LANES, (block + 1) * LANES)
        gin_ref[:, :, lanes] = (
            cot_ref[:, :, lanes].astype(f32) + stencil(lanes, True)
        ).astype(bf16)
        sum_turn(block)
        if block == 1:
            scatter_turn(2, steps - 3)
            scatter_turn(1, steps - 4)
    pending = []
    for part in range(parts):
        for step in range(steps - 5 + max(part - 1, 0), -1, -1):
            pending.append((part, step))
    pending.sort(key=lambda turn: -turn[1])
    for step in range(blocks, steps):
        for turn in pending[:2]:
            scatter_turn(*turn)
        pending = pending[2:]
        sum_turn(step)
    for turn in pending:
        scatter_turn(*turn)
    share_copy().wait()
    for part in range(parts):
        at = slice(part * unit_rows, (part + 1) * unit_rows)
        own = total[part, :, pl.ds(places[part], 1)]
        gwin_ref[at, :] = own[0, 0]
        gwout_ref[at, :] = own[1, 0]
    everything = sums_all[...].reshape(64, channels)
    small_ref[...] = everything[0:53]
    gbin_ref[...] = everything[53:57]


def write_out(*refs):
    count = (len(refs) - 2) // 2
    sources, targets, line, sems = refs[:count], refs[count : 2 * count], refs[-2], refs[-1]
    copies = []
    for at in range(count):
        source = sources[at]
        if at == count - 1:
            size = source.shape[1]
            for row in range(source.shape[0]):
                line[row * size : (row + 1) * size] = source[row]
            source = line
        copies.append(pltpu.make_async_copy(source, targets[at], sems.at[at]))
        copies[-1].start()
    for copy in copies:
        copy.wait()


def on_device(
    rows,
    cols,
    feature_map,
    kernel,
    ln_gain,
    ln_bias,
    w_in,
    b_in,
    w_out,
    b_out,
    layer_scale,
    cotangent,
):
    devices = rows * cols
    parts = 3
    height, width, channels = feature_map.shape
    units = w_out.shape[0]
    steps = devices.bit_length() - 1
    if units % (16 * parts) or devices != 2**steps or steps < 5 or devices * units != 4 * channels:
        return spread_plan(
            feature_map, kernel, ln_gain, ln_bias, w_in, b_in, w_out, b_out, layer_scale, cotangent
        )
    orders = bit_orders(rows, cols)
    piece = units // parts
    pixels = height * width
    f32, bf16 = jnp.float32, jnp.bfloat16
    padded_shape = (height + 6, width + 2 * EDGE, channels)
    outs = pl.pallas_call(
        functools.partial(fused_kernel, rows, cols, orders),
        out_shape=(
            jax.ShapeDtypeStruct(feature_map.shape, bf16),
            jax.ShapeDtypeStruct(feature_map.shape, bf16),
            jax.ShapeDtypeStruct((units, channels), f32),
            jax.ShapeDtypeStruct((units, channels), f32),
            jax.ShapeDtypeStruct((53, channels), f32),
            jax.ShapeDtypeStruct((4, channels), f32),
        ),
        in_specs=[pl.BlockSpec(memory_space=pl.ANY)] * 10,
        out_specs=(pl.BlockSpec(memory_space=pltpu.VMEM),) * 6,
        scratch_shapes=[
            pltpu.VMEM(cotangent.shape, bf16),
            pltpu.VMEM(kernel.shape, f32),
            pltpu.VMEM((channels,), f32),
            pltpu.VMEM((channels,), f32),
            pltpu.VMEM(b_in.shape, f32),
            pltpu.VMEM((channels,), f32),
            pltpu.VMEM((channels,), f32),
            pltpu.VMEM(padded_shape, bf16),
            pltpu.VMEM(padded_shape, bf16),
            pltpu.VMEM((height + 6, width + 16, channels), f32),
            pltpu.VMEM((pixels, channels), f32),
            pltpu.VMEM((pixels, channels), f32),
            pltpu.VMEM((pixels, channels), bf16),
            pltpu.VMEM((pixels, channels), bf16),
            pltpu.VMEM((pixels, channels), f32),
            pltpu.VMEM((pixels, channels), f32),
            pltpu.VMEM((parts, 2, devices, piece, channels), bf16),
            pltpu.VMEM((parts, 2, devices, piece, channels), f32),
            pltpu.VMEM((parts, 2, devices, piece, channels), bf16),
            pltpu.VMEM((parts, 2, devices, piece, channels), bf16),
            pltpu.VMEM((4, 16, channels), f32),
            pltpu.VMEM((2, 16, channels), f32),
            pltpu.VMEM((steps - 1, 2, 16, channels), f32),
            pltpu.VMEM((steps - 1, 2, 16, channels), f32),
            pltpu.VMEM((4, 16, channels), f32),
            pltpu.SemaphoreType.DMA((2 * parts + 8,)),
            pltpu.SemaphoreType.DMA((2, len(SIDES))),
            pltpu.SemaphoreType.DMA((2, len(SIDES))),
            pltpu.SemaphoreType.DMA((parts, steps)),
            pltpu.SemaphoreType.DMA((parts, steps)),
            pltpu.SemaphoreType.DMA((parts, steps)),
            pltpu.SemaphoreType.DMA((parts, steps)),
            pltpu.SemaphoreType.DMA((2 * steps,)),
            pltpu.SemaphoreType.DMA((2 * steps,)),
        ],
        compiler_params=pltpu.CompilerParams(
            collective_id=0, has_side_effects=True, vmem_limit_bytes=50 * 2**20
        ),
        name="convnext_block",
    )(
        feature_map,
        kernel,
        ln_gain,
        ln_bias,
        w_in.T,
        b_in,
        w_out,
        b_out,
        layer_scale,
        cotangent,
    )
    outs = pl.pallas_call(
        write_out,
        out_shape=tuple(jax.ShapeDtypeStruct(out.shape, out.dtype) for out in outs[:-1])
        + (jax.ShapeDtypeStruct(b_in.shape, f32),),
        in_specs=[pl.BlockSpec(memory_space=pltpu.VMEM)] * 6,
        out_specs=(pl.BlockSpec(memory_space=pl.ANY),) * 6,
        scratch_shapes=[pltpu.VMEM(b_in.shape, f32), pltpu.SemaphoreType.DMA((6,))],
        name="write_out",
    )(*outs)
    block_out, grad_input, grad_win, grad_wout, small_grads, grad_b_in = outs
    return (block_out, grad_input, grad_win.T, grad_wout, small_grads, grad_b_in)


def solution(mesh):
    placed = (
        P("row", "col", None),
        P(),
        P(),
        P(),
        P(None, ("row", "col")),
        P(),
        P(("row", "col"), None),
        P(),
        P(),
        P("row", "col", None),
    )
    return jax.shard_map(
        functools.partial(on_device, mesh.shape["row"], mesh.shape["col"]),
        mesh=mesh,
        in_specs=placed,
        out_specs=(
            P("row", "col", None),
            P("row", "col", None),
            P(None, ("row", "col")),
            P(("row", "col"), None),
            P(),
            P(),
        ),
        check_vma=False,
    )
```

```python
import functools
import math

import jax
import jax.numpy as jnp
from jax import lax
from jax.experimental import pallas as pl
from jax.experimental.pallas import tpu as pltpu
from jax.sharding import PartitionSpec as P


def padded_2(x, sides, width):
    for axis, dim in sides:
        peers, length = (lax.axis_size(axis), x.shape[dim])
        up = [(i, (i + 1) % peers) for i in range(peers - 1)]
        down = [(j, i) for i, j in up]
        last = lax.slice_in_dim(x, length - width, length, axis=dim)
        first = lax.slice_in_dim(x, 0, width, axis=dim)
        before = lax.ppermute(last, axis, up)
        after = lax.ppermute(first, axis, down)
        x = jnp.concatenate([before, x, after], axis=dim)
    return x


def gelu_parts(hidden):
    normal_cdf = 0.5 * (1.0 + jax.scipy.special.erf(hidden * (1.0 / math.sqrt(2.0))))
    density = jnp.exp(-0.5 * hidden * hidden) * (1.0 / math.sqrt(2.0 * math.pi))
    return (hidden * normal_cdf, normal_cdf + hidden * density)


def extend(field):
    return padded_2(field, (("row", 0), ("col", 1)), 3)


def spread_plan(
    feature_map, kernel, ln_gain, ln_bias, w_in, b_in, w_out, b_out, layer_scale, cotangent
):
    row_count, col_count, channels = feature_map.shape
    pixels = row_count * col_count
    padded = extend(feature_map).astype(jnp.float32)
    conv = jnp.zeros((row_count, col_count, channels), jnp.float32)
    for tap_row in range(7):
        for tap_col in range(7):
            conv = (
                conv
                + padded[tap_row : tap_row + row_count, tap_col : tap_col + col_count]
                * kernel[tap_row, tap_col]
            )
    average = jnp.mean(conv, -1, keepdims=True)
    centered = conv - average
    variance = jnp.mean(centered * centered, -1, keepdims=True)
    inv_std = lax.rsqrt(variance + 1e-06)
    unit_scaled = centered * inv_std
    normed = (unit_scaled * ln_gain + ln_bias).astype(jnp.bfloat16).reshape(pixels, channels)
    contract_last = (((1,), (1,)), ((), ()))
    contract_first = (((0,), (0,)), ((), ()))
    w_in_full = lax.all_gather(w_in, ("row", "col"), axis=1, tiled=True)
    w_out_full = lax.all_gather(w_out, ("row", "col"), axis=0, tiled=True)
    hidden = jnp.dot(normed, w_in_full, preferred_element_type=jnp.float32) + b_in
    act_value, slope = gelu_parts(hidden)
    activated = act_value.astype(jnp.bfloat16)
    mixed = jnp.dot(activated, w_out_full, preferred_element_type=jnp.float32) + b_out
    source = feature_map.astype(jnp.float32).reshape(pixels, channels)
    block_out = (
        (source + layer_scale * mixed).astype(jnp.bfloat16).reshape(row_count, col_count, channels)
    )
    grad_flow = cotangent.astype(jnp.float32).reshape(pixels, channels)
    grad_mixed = grad_flow * layer_scale
    mixed_low = grad_mixed.astype(jnp.bfloat16)
    grad_act = lax.dot_general(
        mixed_low, w_out_full, contract_last, preferred_element_type=jnp.float32
    )
    grad_hidden = (grad_act * slope).astype(jnp.bfloat16)
    grad_w_out = lax.psum_scatter(
        lax.dot_general(activated, mixed_low, contract_first, preferred_element_type=jnp.float32),
        ("row", "col"),
        scatter_dimension=0,
        tiled=True,
    )
    win_term = lax.dot_general(
        normed, grad_hidden, contract_first, preferred_element_type=jnp.float32
    )
    grad_w_in = lax.psum_scatter(win_term, ("row", "col"), scatter_dimension=1, tiled=True)
    grad_normed = lax.dot_general(
        grad_hidden, w_in_full, contract_last, preferred_element_type=jnp.float32
    )
    grad_normed = grad_normed.reshape(row_count, col_count, channels)
    grad_gain = jnp.sum(grad_normed * unit_scaled, (0, 1))
    grad_lnb = jnp.sum(grad_normed, (0, 1))
    scaled_grad = grad_normed * ln_gain
    grad_conv = inv_std * (
        scaled_grad
        - jnp.mean(scaled_grad, -1, keepdims=True)
        - unit_scaled * jnp.mean(scaled_grad * unit_scaled, -1, keepdims=True)
    )
    tap_terms = []
    for tap_row in range(7):
        for tap_col in range(7):
            tap_terms.append(
                jnp.sum(
                    padded[tap_row : tap_row + row_count, tap_col : tap_col + col_count]
                    * grad_conv,
                    (0, 1),
                )
            )
    grad_pad = extend(grad_conv.astype(jnp.bfloat16)).astype(jnp.float32)
    back_conv = jnp.zeros((row_count, col_count, channels), jnp.float32)
    for tap_row in range(7):
        for tap_col in range(7):
            back_conv = (
                back_conv
                + grad_pad[
                    6 - tap_row : 6 - tap_row + row_count, 6 - tap_col : 6 - tap_col + col_count
                ]
                * kernel[tap_row, tap_col]
            )
    grad_input = (cotangent.astype(jnp.float32) + back_conv).astype(jnp.bfloat16)
    small_local = jnp.concatenate(
        [
            jnp.stack(tap_terms, 0),
            grad_gain[None],
            grad_lnb[None],
            jnp.sum(grad_mixed, 0)[None],
            jnp.sum(grad_flow * mixed, 0)[None],
        ],
        0,
    )
    bias_local = jnp.sum(grad_hidden.astype(jnp.float32), 0)
    small_grads, grad_b_in = lax.psum((small_local, bias_local), ("row", "col"))
    return (block_out, grad_input, grad_w_in, grad_w_out, small_grads, grad_b_in)


MESH = pl.DeviceIdType.MESH
SIDES = [(a, b) for a in (-1, 0, 1) for b in (-1, 0, 1) if (a, b) != (0, 0)]
EDGE = 16
TILE = 32
LANES = 128
CONTRACT_LAST = (((1,), (1,)), ((), ()))
CONTRACT_FIRST = (((0,), (0,)), ((), ()))


def bit_orders(rows, cols):
    bits = (rows * cols).bit_length() - 1
    pair = cols.bit_length() - 1
    rest = [b for b in range(bits - 1, -1, -1) if b != pair]
    orders = [rest, rest[-1:] + rest[:-1], rest[-2:] + rest[:-2]]
    return [order + [pair] for order in orders]


def fused_kernel(
    rows,
    cols,
    orders,
    x_hbm,
    taps_hbm,
    gain_hbm,
    offset_hbm,
    win_hbm,
    bin_hbm,
    wout_hbm,
    bout_hbm,
    scale_hbm,
    cot_hbm,
    out_hbm,
    gin_hbm,
    gwin_hbm,
    gwout_hbm,
    small_hbm,
    gbin_hbm,
    out_ref,
    gin_ref,
    gwin_ref,
    gwout_ref,
    small_ref,
    gbin_ref,
    hid,
    gact,
    act,
    ghid,
    inv,
    cot_ref,
    taps_ref,
    gain_ref,
    offset_ref,
    bin_ref,
    bout_ref,
    scale_ref,
    xpad,
    gpad,
    wide,
    conv,
    unit,
    normed,
    mixed_low,
    mixed,
    gnorm,
    weights,
    total,
    leaving,
    arriving,
    sums,
    sums_first,
    sums_run,
    sums_in,
    sums_all,
    local_sem,
    halo_send,
    halo_recv,
    gather_send,
    gather_recv,
    scatter_send,
    scatter_recv,
    sum_send,
    sum_recv,
):
    height, width, channels = cot_ref.shape
    pixels = height * width
    parts = len(orders)
    steps = len(orders[0])
    unit_rows = weights.shape[3]
    chunk = weights.shape[2] * unit_rows
    row, col = lax.axis_index("row"), lax.axis_index("col")
    me = row * cols + col
    f32, bf16 = jnp.float32, jnp.bfloat16

    def bit_of(b):
        return lax.rem(lax.div(me, 2**b), 2)

    def partner(b):
        other = me + (1 - 2 * bit_of(b)) * 2**b
        return (lax.div(other, cols), lax.rem(other, cols))

    places = []
    for order in orders:
        place = 0
        for step, b in enumerate(order):
            place = place + bit_of(b) * 2**step
        places.append(place)

    def exists(side):
        dr, dc = side
        there = None
        for delta, at, count in ((dr, row, rows), (dc, col, cols)):
            if delta:
                ok = at > 0 if delta < 0 else at < count - 1
                there = ok if there is None else jnp.logical_and(there, ok)
        return there

    def halo_copy(source, pad, which, side, receiving):
        dr, dc = side
        at = SIDES.index(side)
        back = SIDES.index((-dr, -dc))
        row_from = {-1: pl.ds(0, 3), 0: pl.ds(0, height), 1: pl.ds(height - 3, 3)}[dr]
        col_from = {-1: pl.ds(0, EDGE), 0: pl.ds(0, width), 1: pl.ds(width - EDGE, EDGE)}[dc]
        into_r, into_c = (dr, dc) if receiving else (-dr, -dc)
        row_to = {-1: pl.ds(0, 3), 0: pl.ds(3, height), 1: pl.ds(height + 3, 3)}[into_r]
        col_to = {-1: pl.ds(0, EDGE), 0: pl.ds(EDGE, width), 1: pl.ds(width + EDGE, EDGE)}[into_c]
        return pltpu.make_async_remote_copy(
            src_ref=source.at[row_from, col_from],
            dst_ref=pad.at[row_to, col_to],
            send_sem=halo_send.at[which, at],
            recv_sem=halo_recv.at[which, back if receiving else at],
            device_id=(row + dr, col + dc),
            device_id_type=MESH,
        )

    def halo_start(source, pad, which):
        for side in SIDES:

            @pl.when(exists(side))
            def _():
                halo_copy(source, pad, which, side, False).start()

    def halo_wait(source, pad, which):
        for side in SIDES:

            @pl.when(exists(side))
            def _():
                halo_copy(source, pad, which, side, False).wait_send()
                halo_copy(source, pad, which, side, True).wait_recv()

    def gather_copy(part, step):
        size = 2**step
        held = weights.at[part, :, pl.ds(lax.div(places[part], size) * size, size)]
        return pltpu.make_async_remote_copy(
            src_ref=held,
            dst_ref=held,
            send_sem=gather_send.at[part, step],
            recv_sem=gather_recv.at[part, step],
            device_id=partner(orders[part][step]),
            device_id_type=MESH,
        )

    def gather_turn(part, step):
        if step:
            gather_copy(part, step - 1).wait()
        if step < steps:
            gather_copy(part, step).start()

    def scatter_copy(part, step):
        size = 2**step
        return pltpu.make_async_remote_copy(
            src_ref=leaving.at[part, :, pl.ds(size, size)],
            dst_ref=arriving.at[part, :, pl.ds(size, size)],
            send_sem=scatter_send.at[part, step],
            recv_sem=scatter_recv.at[part, step],
            device_id=partner(orders[part][step]),
            device_id_type=MESH,
        )

    def scatter_start(part, step):
        size = 2**step
        mine = lax.div(places[part], size)
        away = (mine + 1 - 2 * lax.rem(mine, 2)) * size
        leaving[part, :, size : 2 * size] = total[part, :, pl.ds(away, size)].astype(bf16)
        scatter_copy(part, step).start()

    def scatter_turn(part, step):
        size = 2**step
        scatter_copy(part, step).wait()
        keep = pl.ds(lax.div(places[part], size) * size, size)
        total[part, :, keep] = total[part, :, keep] + arriving[part, :, size : 2 * size].astype(f32)
        if step:
            scatter_start(part, step - 1)

    pair_bit = orders[0][-1]
    pair_half = bit_of(pair_bit)
    sum_orders = [orders[0][:-1], orders[0][:-1][::-1]]

    def pair_copy():
        return pltpu.make_async_remote_copy(
            src_ref=sums.at[pl.ds((1 - pair_half) * 2, 2)],
            dst_ref=sums_first,
            send_sem=sum_send.at[0],
            recv_sem=sum_recv.at[0],
            device_id=partner(pair_bit),
            device_id_type=MESH,
        )

    def run_copy(step, half):
        return pltpu.make_async_remote_copy(
            src_ref=sums_run.at[step, half],
            dst_ref=sums_in.at[step, half],
            send_sem=sum_send.at[1 + 2 * step + half],
            recv_sem=sum_recv.at[1 + 2 * step + half],
            device_id=partner(sum_orders[half][step]),
            device_id_type=MESH,
        )

    def share_copy():
        own = sums_all.at[pl.ds(pair_half * 2, 2)]
        return pltpu.make_async_remote_copy(
            src_ref=own,
            dst_ref=own,
            send_sem=sum_send.at[2 * steps - 1],
            recv_sem=sum_recv.at[2 * steps - 1],
            device_id=partner(pair_bit),
            device_id_type=MESH,
        )

    def sum_turn(step):
        last = steps - 1
        if step == 0:
            pair_copy().wait()
            sums_run[0] = sums[pl.ds(pair_half * 2, 2)] + sums_first[...]
        else:
            for half in range(2):
                run_copy(step - 1, half).wait()
                added = sums_run[step - 1, half] + sums_in[step - 1, half]
                if step < last:
                    sums_run[step, half] = added
                    run_copy(step, half).start()
                else:
                    sums_all[pl.ds(pair_half * 2 + half, 1)] = added[None]
            if step == last:
                share_copy().start()
            return
        for half in range(2):
            run_copy(0, half).start()

    given = []

    def give(source, target):
        at = 2 * parts + 8 + len(given)
        given.append(pltpu.make_async_copy(source, target, local_sem.at[at]))
        given[-1].start()

    def put_sum(at, lanes, value):
        sums[at // 16, at % 16 : at % 16 + 1, lanes] = value

    every = slice(0, channels)
    xpad[...] = jnp.zeros_like(xpad)
    center = xpad.at[pl.ds(3, height), pl.ds(EDGE, width)]
    moves = []
    for part in range(parts):
        for which, source in enumerate((win_hbm, wout_hbm)):
            moves.append(
                (source.at[pl.ds(part * unit_rows, unit_rows)], weights.at[part, which, places[part]])
            )
    moves += [
        (x_hbm, center),
        (cot_hbm, cot_ref),
        (scale_hbm, scale_ref),
        (taps_hbm, taps_ref),
        (bin_hbm, bin_ref),
        (gain_hbm, gain_ref),
        (offset_hbm, offset_ref),
        (bout_hbm, bout_ref),
    ]
    moves = [
        pltpu.make_async_copy(source, target, local_sem.at[at])
        for at, (source, target) in enumerate(moves)
    ]
    for move in moves:
        move.start()
    gpad[...] = jnp.zeros_like(gpad)

    barrier = pltpu.get_barrier_semaphore()
    expected = steps
    for b in range(steps):
        pl.semaphore_signal(barrier, inc=1, device_id=partner(b), device_id_type=MESH)
    for side in SIDES:
        here = exists(side)
        expected = expected + jnp.where(here, 1, 0)

        @pl.when(here)
        def _():
            pl.semaphore_signal(
                barrier, inc=1, device_id=(row + side[0], col + side[1]), device_id_type=MESH
            )

    pl.semaphore_wait(barrier, expected)

    halo_start(x_hbm, xpad, 0)
    for move in moves[: 2 * parts]:
        move.wait()
    for part in range(parts):
        gather_turn(part, 0)
    for move in moves[2 * parts :]:
        move.wait()

    def as_row(ref):
        return ref[...].reshape(1, ref.shape[0])

    gain, offset = as_row(gain_ref), as_row(offset_ref)
    out_bias, scale = as_row(bout_ref), as_row(scale_ref)
    sums[3] = jnp.zeros((16, channels), f32)
    grad_mixed = cot_ref[...].astype(f32).reshape(pixels, channels) * scale
    mixed_low[...] = grad_mixed.astype(bf16)
    put_sum(51, every, jnp.sum(grad_mixed, 0, keepdims=True))

    owners = []
    for order in orders:
        owners.append(
            [
                sum(((place >> step) & 1) << b for step, b in enumerate(order))
                for place in range(2**steps)
            ]
        )
    bias_all = as_row(bin_ref)
    biases = []
    for part in range(parts):
        starts = [(owner * parts + part) * unit_rows for owner in owners[part]]
        biases.append(
            jnp.concatenate([bias_all[:, at : at + unit_rows] for at in starts], 1)
        )

    halo_wait(x_hbm, xpad, 0)
    for part in range(parts):
        gather_turn(part, 1)
    wide[...] = xpad[:, 8 : width + 24].astype(f32)

    def window(shift, lanes):
        return wide[:, 5 + shift : 5 + shift + width, lanes]

    def stencil(lanes, flip):
        result = jnp.zeros((height, width, LANES), f32)
        for tap_col in range(7):
            shifted = window(tap_col, lanes)
            for tap_row in range(7):
                a, b = (6 - tap_row, 6 - tap_col) if flip else (tap_row, tap_col)
                result = result + shifted[tap_row : tap_row + height] * taps_ref[a, b : b + 1, lanes]
        return result

    blocks = channels // LANES
    for block in range(blocks):
        lanes = slice(block * LANES, (block + 1) * LANES)
        conv[:, lanes] = stencil(lanes, False).reshape(pixels, LANES)
        if block + 2 < steps:
            for part in range(parts):
                gather_turn(part, block + 2)

    def norm_tile(tile, carry):
        at = pl.ds(pl.multiple_of(tile * TILE, TILE), TILE)
        centered = conv[at, :]
        centered = centered - jnp.mean(centered, -1, keepdims=True)
        inv_std = lax.rsqrt(jnp.mean(centered * centered, -1, keepdims=True) + 1e-06)
        unit_scaled = centered * inv_std
        inv[at, :] = inv_std
        unit[at, :] = unit_scaled
        normed[at, :] = (unit_scaled * gain + offset).astype(bf16)
        return carry

    lax.fori_loop(0, pixels // TILE, norm_tile, 0)
    for step in range(blocks + 2, steps):
        for part in range(parts):
            gather_turn(part, step)

    bias_sums = []
    for part in range(parts):
        gather_turn(part, steps)
        win = weights[part, 0].reshape(chunk, channels)
        wout = weights[part, 1].reshape(chunk, channels)
        hid[...] = lax.dot_general(normed[...], win, CONTRACT_LAST, preferred_element_type=f32)
        gact[...] = lax.dot_general(
            mixed_low[...], wout, CONTRACT_LAST, preferred_element_type=f32
        )

        def gelu_tile(tile, bias_sum):
            at = pl.ds(pl.multiple_of(tile * 16, 16), 16)
            act_value, slope = gelu_parts(hid[at, :] + biases[part])
            act[at, :] = act_value.astype(bf16)
            low = (gact[at, :] * slope).astype(bf16)
            ghid[at, :] = low
            return bias_sum + low.astype(f32)

        bias_sum = lax.fori_loop(
            0, pixels // 16, gelu_tile, jnp.zeros((16, chunk), f32)
        )
        bias_sums.append(jnp.sum(bias_sum, 0, keepdims=True))
        activated, grad_hidden = act[...], ghid[...]
        total[part, 1] = lax.dot_general(
            activated, mixed_low[...], CONTRACT_FIRST, preferred_element_type=f32
        ).reshape(-1, unit_rows, channels)
        total[part, 0] = lax.dot_general(
            grad_hidden, normed[...], CONTRACT_FIRST, preferred_element_type=f32
        ).reshape(-1, unit_rows, channels)
        scatter_start(part, steps - 1)
        mixed_term = jnp.dot(activated, wout, preferred_element_type=f32)
        gnorm_term = jnp.dot(grad_hidden, win, preferred_element_type=f32)
        mixed[...] = mixed_term if part == 0 else mixed[...] + mixed_term
        gnorm[...] = gnorm_term if part == 0 else gnorm[...] + gnorm_term
        if part:
            scatter_turn(part - 1, steps - 1)

    def back_tile(tile, carry):
        gain_sum, offset_sum = carry
        at = pl.ds(pl.multiple_of(tile * TILE, TILE), TILE)
        grad_normed = gnorm[at, :]
        unit_scaled = unit[at, :]
        product = grad_normed * unit_scaled
        scaled = grad_normed * gain
        grad_conv = inv[at, :] * (
            scaled
            - jnp.mean(scaled, -1, keepdims=True)
            - unit_scaled * jnp.mean(scaled * unit_scaled, -1, keepdims=True)
        )
        conv[at, :] = grad_conv
        normed[at, :] = grad_conv.astype(bf16)
        return (
            gain_sum + jnp.sum(product, 0, keepdims=True),
            offset_sum + jnp.sum(grad_normed, 0, keepdims=True),
        )

    none = jnp.zeros((1, channels), f32)
    gain_sum, offset_sum = lax.fori_loop(0, pixels // TILE, back_tile, (none, none))
    put_sum(49, every, gain_sum)
    put_sum(50, every, offset_sum)
    gpad[3 : 3 + height, EDGE : EDGE + width] = normed[...].reshape(height, width, channels)
    grad_block = gpad.at[pl.ds(3, height), pl.ds(EDGE, width)]
    halo_start(grad_block, gpad, 1)
    scatter_turn(2, steps - 1)

    mixed_full = mixed[...] + out_bias
    source = center[...].astype(f32).reshape(pixels, channels)
    out_ref[...] = (source + scale * mixed_full).astype(bf16).reshape(height, width, channels)
    grad_flow = cot_ref[...].astype(f32).reshape(pixels, channels)
    put_sum(52, every, jnp.sum(grad_flow * mixed_full, 0, keepdims=True))
    for line in range(4):
        pieces = []
        for owner in range(line * 2**steps // 4, (line + 1) * 2**steps // 4):
            for part in range(parts):
                at = owners[part].index(owner) * unit_rows
                pieces.append(bias_sums[part][:, at : at + unit_rows])
        put_sum(53 + line, every, jnp.concatenate(pieces, 1))
    give(out_ref, out_hbm)

    for block in range(blocks):
        lanes = slice(block * LANES, (block + 1) * LANES)
        grad_part = conv[:, lanes].reshape(height, width, LANES)
        for tap_col in range(7):
            shifted = window(tap_col, lanes)
            for tap_row in range(7):
                at = tap_row * 7 + tap_col
                term = shifted[tap_row : tap_row + height] * grad_part
                put_sum(at, lanes, jnp.sum(term.reshape(pixels, LANES), 0, keepdims=True))
        if block == 0:
            scatter_turn(0, steps - 2)
            scatter_turn(1, steps - 2)
    pair_copy().start()
    for part in (2, 0, 1):
        scatter_turn(part, steps - 2 if part == 2 else steps - 3)

    halo_wait(grad_block, gpad, 1)
    wide[...] = gpad[:, 8 : width + 24].astype(f32)
    for block in range(blocks):
        lanes = slice(block * LANES, (block + 1) * LANES)
        gin_ref[:, :, lanes] = (
            cot_ref[:, :, lanes].astype(f32) + stencil(lanes, True)
        ).astype(bf16)
        sum_turn(block)
        if block == 1:
            scatter_turn(2, steps - 3)
    give(gin_ref, gin_hbm)
    turn = steps - 4
    for step in range(blocks, steps):
        if turn >= 0:
            for part in range(parts):
                scatter_turn(part, turn)
            turn -= 1
        sum_turn(step)
    for step in range(turn, -1, -1):
        for part in range(parts):
            scatter_turn(part, step)
    for part in range(parts):
        at = slice(part * unit_rows, (part + 1) * unit_rows)
        own = total[part, :, pl.ds(places[part], 1)]
        gwin_ref[at, :] = own[0, 0]
        gwout_ref[at, :] = own[1, 0]
    give(gwin_ref, gwin_hbm)
    give(gwout_ref, gwout_hbm)
    share_copy().wait()
    everything = sums_all[...].reshape(64, channels)
    small_ref[...] = everything[0:53]
    for line in range(4):
        gbin_ref[line * channels : (line + 1) * channels] = everything[53 + line]
    give(small_ref, small_hbm)
    give(gbin_ref, gbin_hbm)
    for move in given:
        move.wait()


def write_out(*refs):
    count = len(refs) // 2
    sems = refs[-1]
    copies = [
        pltpu.make_async_copy(refs[at], refs[count + at], sems.at[at]) for at in range(count)
    ]
    for copy in copies:
        copy.start()
    for copy in copies:
        copy.wait()


def on_device(
    rows,
    cols,
    feature_map,
    kernel,
    ln_gain,
    ln_bias,
    w_in,
    b_in,
    w_out,
    b_out,
    layer_scale,
    cotangent,
):
    devices = rows * cols
    parts = 3
    height, width, channels = feature_map.shape
    units = w_out.shape[0]
    steps = devices.bit_length() - 1
    if units % (16 * parts) or devices != 2**steps or steps < 5 or devices * units != 4 * channels:
        return spread_plan(
            feature_map, kernel, ln_gain, ln_bias, w_in, b_in, w_out, b_out, layer_scale, cotangent
        )
    orders = bit_orders(rows, cols)
    piece = units // parts
    pixels = height * width
    f32, bf16 = jnp.float32, jnp.bfloat16
    padded_shape = (height + 6, width + 2 * EDGE, channels)
    outs = pl.pallas_call(
        functools.partial(fused_kernel, rows, cols, orders),
        out_shape=(
            jax.ShapeDtypeStruct(feature_map.shape, bf16),
            jax.ShapeDtypeStruct(feature_map.shape, bf16),
            jax.ShapeDtypeStruct((units, channels), f32),
            jax.ShapeDtypeStruct((units, channels), f32),
            jax.ShapeDtypeStruct((53, channels), f32),
            jax.ShapeDtypeStruct(b_in.shape, f32),
        ),
        in_specs=[pl.BlockSpec(memory_space=pltpu.HBM)] * 10,
        out_specs=(pl.BlockSpec(memory_space=pltpu.HBM),) * 6,
        scratch_shapes=[
            pltpu.VMEM(cotangent.shape, bf16),
            pltpu.VMEM(cotangent.shape, bf16),
            pltpu.VMEM((units, channels), f32),
            pltpu.VMEM((units, channels), f32),
            pltpu.VMEM((53, channels), f32),
            pltpu.VMEM(b_in.shape, f32),
            pltpu.VMEM((pixels, devices * piece), f32),
            pltpu.VMEM((pixels, devices * piece), f32),
            pltpu.VMEM((pixels, devices * piece), bf16),
            pltpu.VMEM((pixels, devices * piece), bf16),
            pltpu.VMEM((pixels, 1), f32),
            pltpu.VMEM(cotangent.shape, bf16),
            pltpu.VMEM(kernel.shape, f32),
            pltpu.VMEM((channels,), f32),
            pltpu.VMEM((channels,), f32),
            pltpu.VMEM(b_in.shape, f32),
            pltpu.VMEM((channels,), f32),
            pltpu.VMEM((channels,), f32),
            pltpu.VMEM(padded_shape, bf16),
            pltpu.VMEM(padded_shape, bf16),
            pltpu.VMEM((height + 6, width + 16, channels), f32),
            pltpu.VMEM((pixels, channels), f32),
            pltpu.VMEM((pixels, channels), f32),
            pltpu.VMEM((pixels, channels), bf16),
            pltpu.VMEM((pixels, channels), bf16),
            pltpu.VMEM((pixels, channels), f32),
            pltpu.VMEM((pixels, channels), f32),
            pltpu.VMEM((parts, 2, devices, piece, channels), bf16),
            pltpu.VMEM((parts, 2, devices, piece, channels), f32),
            pltpu.VMEM((parts, 2, devices, piece, channels), bf16),
            pltpu.VMEM((parts, 2, devices, piece, channels), bf16),
            pltpu.VMEM((4, 16, channels), f32),
            pltpu.VMEM((2, 16, channels), f32),
            pltpu.VMEM((steps - 1, 2, 16, channels), f32),
            pltpu.VMEM((steps - 1, 2, 16, channels), f32),
            pltpu.VMEM((4, 16, channels), f32),
            pltpu.SemaphoreType.DMA((2 * parts + 14,)),
            pltpu.SemaphoreType.DMA((2, len(SIDES))),
            pltpu.SemaphoreType.DMA((2, len(SIDES))),
            pltpu.SemaphoreType.DMA((parts, steps)),
            pltpu.SemaphoreType.DMA((parts, steps)),
            pltpu.SemaphoreType.DMA((parts, steps)),
            pltpu.SemaphoreType.DMA((parts, steps)),
            pltpu.SemaphoreType.DMA((2 * steps,)),
            pltpu.SemaphoreType.DMA((2 * steps,)),
        ],
        compiler_params=pltpu.CompilerParams(
            collective_id=0, has_side_effects=True, vmem_limit_bytes=60 * 2**20
        ),
        name="convnext_block",
    )(
        feature_map,
        kernel,
        ln_gain,
        ln_bias,
        w_in.T,
        b_in,
        w_out,
        b_out,
        layer_scale,
        cotangent,
    )
    outs = pl.pallas_call(
        write_out,
        out_shape=tuple(jax.ShapeDtypeStruct(out.shape, out.dtype) for out in outs),
        in_specs=[pl.BlockSpec(memory_space=pltpu.HBM)] * 6,
        out_specs=(pl.BlockSpec(memory_space=pltpu.HBM),) * 6,
        scratch_shapes=[pltpu.SemaphoreType.DMA((6,))],
        compiler_params=pltpu.CompilerParams(vmem_limit_bytes=60 * 2**20),
        name="write_out",
    )(*outs)
    block_out, grad_input, grad_win, grad_wout, small_grads, grad_b_in = outs
    return (block_out, grad_input, grad_win.T, grad_wout, small_grads, grad_b_in)


def solution(mesh):
    placed = (
        P("row", "col", None),
        P(),
        P(),
        P(),
        P(None, ("row", "col")),
        P(),
        P(("row", "col"), None),
        P(),
        P(),
        P("row", "col", None),
    )
    return jax.shard_map(
        functools.partial(on_device, mesh.shape["row"], mesh.shape["col"]),
        mesh=mesh,
        in_specs=placed,
        out_specs=(
            P("row", "col", None),
            P("row", "col", None),
            P(None, ("row", "col")),
            P(("row", "col"), None),
            P(),
            P(),
        ),
        check_vma=False,
    )
```

```python
import functools
import math

import jax
import jax.numpy as jnp
from jax import lax
from jax.experimental import pallas as pl
from jax.experimental.pallas import tpu as pltpu
from jax.sharding import PartitionSpec as P


def padded_2(x, sides, width):
    for axis, dim in sides:
        peers, length = (lax.axis_size(axis), x.shape[dim])
        up = [(i, (i + 1) % peers) for i in range(peers - 1)]
        down = [(j, i) for i, j in up]
        last = lax.slice_in_dim(x, length - width, length, axis=dim)
        first = lax.slice_in_dim(x, 0, width, axis=dim)
        before = lax.ppermute(last, axis, up)
        after = lax.ppermute(first, axis, down)
        x = jnp.concatenate([before, x, after], axis=dim)
    return x


def gelu_parts(hidden):
    normal_cdf = 0.5 * (1.0 + jax.scipy.special.erf(hidden * (1.0 / math.sqrt(2.0))))
    density = jnp.exp(-0.5 * hidden * hidden) * (1.0 / math.sqrt(2.0 * math.pi))
    return (hidden * normal_cdf, normal_cdf + hidden * density)


def extend(field):
    return padded_2(field, (("row", 0), ("col", 1)), 3)


def spread_plan(
    feature_map, kernel, ln_gain, ln_bias, w_in, b_in, w_out, b_out, layer_scale, cotangent
):
    row_count, col_count, channels = feature_map.shape
    pixels = row_count * col_count
    padded = extend(feature_map).astype(jnp.float32)
    conv = jnp.zeros((row_count, col_count, channels), jnp.float32)
    for tap_row in range(7):
        for tap_col in range(7):
            conv = (
                conv
                + padded[tap_row : tap_row + row_count, tap_col : tap_col + col_count]
                * kernel[tap_row, tap_col]
            )
    average = jnp.mean(conv, -1, keepdims=True)
    centered = conv - average
    variance = jnp.mean(centered * centered, -1, keepdims=True)
    inv_std = lax.rsqrt(variance + 1e-06)
    unit_scaled = centered * inv_std
    normed = (unit_scaled * ln_gain + ln_bias).astype(jnp.bfloat16).reshape(pixels, channels)
    contract_last = (((1,), (1,)), ((), ()))
    contract_first = (((0,), (0,)), ((), ()))
    w_in_full = lax.all_gather(w_in, ("row", "col"), axis=1, tiled=True)
    w_out_full = lax.all_gather(w_out, ("row", "col"), axis=0, tiled=True)
    hidden = jnp.dot(normed, w_in_full, preferred_element_type=jnp.float32) + b_in
    act_value, slope = gelu_parts(hidden)
    activated = act_value.astype(jnp.bfloat16)
    mixed = jnp.dot(activated, w_out_full, preferred_element_type=jnp.float32) + b_out
    source = feature_map.astype(jnp.float32).reshape(pixels, channels)
    block_out = (
        (source + layer_scale * mixed).astype(jnp.bfloat16).reshape(row_count, col_count, channels)
    )
    grad_flow = cotangent.astype(jnp.float32).reshape(pixels, channels)
    grad_mixed = grad_flow * layer_scale
    mixed_low = grad_mixed.astype(jnp.bfloat16)
    grad_act = lax.dot_general(
        mixed_low, w_out_full, contract_last, preferred_element_type=jnp.float32
    )
    grad_hidden = (grad_act * slope).astype(jnp.bfloat16)
    grad_w_out = lax.psum_scatter(
        lax.dot_general(activated, mixed_low, contract_first, preferred_element_type=jnp.float32),
        ("row", "col"),
        scatter_dimension=0,
        tiled=True,
    )
    win_term = lax.dot_general(
        normed, grad_hidden, contract_first, preferred_element_type=jnp.float32
    )
    grad_w_in = lax.psum_scatter(win_term, ("row", "col"), scatter_dimension=1, tiled=True)
    grad_normed = lax.dot_general(
        grad_hidden, w_in_full, contract_last, preferred_element_type=jnp.float32
    )
    grad_normed = grad_normed.reshape(row_count, col_count, channels)
    grad_gain = jnp.sum(grad_normed * unit_scaled, (0, 1))
    grad_lnb = jnp.sum(grad_normed, (0, 1))
    scaled_grad = grad_normed * ln_gain
    grad_conv = inv_std * (
        scaled_grad
        - jnp.mean(scaled_grad, -1, keepdims=True)
        - unit_scaled * jnp.mean(scaled_grad * unit_scaled, -1, keepdims=True)
    )
    tap_terms = []
    for tap_row in range(7):
        for tap_col in range(7):
            tap_terms.append(
                jnp.sum(
                    padded[tap_row : tap_row + row_count, tap_col : tap_col + col_count]
                    * grad_conv,
                    (0, 1),
                )
            )
    grad_pad = extend(grad_conv.astype(jnp.bfloat16)).astype(jnp.float32)
    back_conv = jnp.zeros((row_count, col_count, channels), jnp.float32)
    for tap_row in range(7):
        for tap_col in range(7):
            back_conv = (
                back_conv
                + grad_pad[
                    6 - tap_row : 6 - tap_row + row_count, 6 - tap_col : 6 - tap_col + col_count
                ]
                * kernel[tap_row, tap_col]
            )
    grad_input = (cotangent.astype(jnp.float32) + back_conv).astype(jnp.bfloat16)
    small_local = jnp.concatenate(
        [
            jnp.stack(tap_terms, 0),
            grad_gain[None],
            grad_lnb[None],
            jnp.sum(grad_mixed, 0)[None],
            jnp.sum(grad_flow * mixed, 0)[None],
        ],
        0,
    )
    bias_local = jnp.sum(grad_hidden.astype(jnp.float32), 0)
    small_grads, grad_b_in = lax.psum((small_local, bias_local), ("row", "col"))
    return (block_out, grad_input, grad_w_in, grad_w_out, small_grads, grad_b_in)


MESH = pl.DeviceIdType.MESH
SIDES = [(a, b) for a in (-1, 0, 1) for b in (-1, 0, 1) if (a, b) != (0, 0)]
EDGE = 16
TILE = 32
LANES = 128
CONTRACT_LAST = (((1,), (1,)), ((), ()))
CONTRACT_FIRST = (((0,), (0,)), ((), ()))


def bit_orders(rows, cols):
    bits = (rows * cols).bit_length() - 1
    pair = cols.bit_length() - 1
    rest = [b for b in range(bits - 1, -1, -1) if b != pair]
    orders = [rest, rest[-1:] + rest[:-1], rest[-2:] + rest[:-2]]
    return [order + [pair] for order in orders]


def fused_kernel(
    rows,
    cols,
    orders,
    x_hbm,
    taps_hbm,
    gain_hbm,
    offset_hbm,
    win_hbm,
    bin_hbm,
    wout_hbm,
    bout_hbm,
    scale_hbm,
    cot_hbm,
    out_ref,
    gin_ref,
    gwin_ref,
    gwout_ref,
    small_ref,
    gbin_ref,
    hid,
    gact,
    act,
    ghid,
    inv,
    cot_ref,
    taps_ref,
    gain_ref,
    offset_ref,
    bin_ref,
    bout_ref,
    scale_ref,
    xpad,
    gpad,
    wide,
    conv,
    unit,
    normed,
    mixed_low,
    mixed,
    gnorm,
    weights,
    total,
    leaving,
    arriving,
    sums,
    sums_first,
    sums_run,
    sums_in,
    sums_all,
    local_sem,
    halo_send,
    halo_recv,
    gather_send,
    gather_recv,
    scatter_send,
    scatter_recv,
    sum_send,
    sum_recv,
):
    height, width, channels = cot_ref.shape
    pixels = height * width
    parts = len(orders)
    steps = len(orders[0])
    unit_rows = weights.shape[3]
    chunk = weights.shape[2] * unit_rows
    row, col = lax.axis_index("row"), lax.axis_index("col")
    me = row * cols + col
    f32, bf16 = jnp.float32, jnp.bfloat16

    def bit_of(b):
        return lax.rem(lax.div(me, 2**b), 2)

    def partner(b):
        other = me + (1 - 2 * bit_of(b)) * 2**b
        return (lax.div(other, cols), lax.rem(other, cols))

    places = []
    for order in orders:
        place = 0
        for step, b in enumerate(order):
            place = place + bit_of(b) * 2**step
        places.append(place)

    def exists(side):
        dr, dc = side
        there = None
        for delta, at, count in ((dr, row, rows), (dc, col, cols)):
            if delta:
                ok = at > 0 if delta < 0 else at < count - 1
                there = ok if there is None else jnp.logical_and(there, ok)
        return there

    def halo_copy(source, pad, which, side, receiving):
        dr, dc = side
        at = SIDES.index(side)
        back = SIDES.index((-dr, -dc))
        row_from = {-1: pl.ds(0, 3), 0: pl.ds(0, height), 1: pl.ds(height - 3, 3)}[dr]
        col_from = {-1: pl.ds(0, EDGE), 0: pl.ds(0, width), 1: pl.ds(width - EDGE, EDGE)}[dc]
        into_r, into_c = (dr, dc) if receiving else (-dr, -dc)
        row_to = {-1: pl.ds(0, 3), 0: pl.ds(3, height), 1: pl.ds(height + 3, 3)}[into_r]
        col_to = {-1: pl.ds(0, EDGE), 0: pl.ds(EDGE, width), 1: pl.ds(width + EDGE, EDGE)}[into_c]
        return pltpu.make_async_remote_copy(
            src_ref=source.at[row_from, col_from],
            dst_ref=pad.at[row_to, col_to],
            send_sem=halo_send.at[which, at],
            recv_sem=halo_recv.at[which, back if receiving else at],
            device_id=(row + dr, col + dc),
            device_id_type=MESH,
        )

    def halo_start(source, pad, which):
        for side in SIDES:

            @pl.when(exists(side))
            def _():
                halo_copy(source, pad, which, side, False).start()

    def halo_wait(source, pad, which):
        for side in SIDES:

            @pl.when(exists(side))
            def _():
                halo_copy(source, pad, which, side, False).wait_send()
                halo_copy(source, pad, which, side, True).wait_recv()

    def gather_copy(part, step):
        size = 2**step
        held = weights.at[part, :, pl.ds(lax.div(places[part], size) * size, size)]
        return pltpu.make_async_remote_copy(
            src_ref=held,
            dst_ref=held,
            send_sem=gather_send.at[part, step],
            recv_sem=gather_recv.at[part, step],
            device_id=partner(orders[part][step]),
            device_id_type=MESH,
        )

    def gather_turn(part, step):
        if step:
            gather_copy(part, step - 1).wait()
        if step < steps:
            gather_copy(part, step).start()

    def scatter_copy(part, step):
        size = 2**step
        return pltpu.make_async_remote_copy(
            src_ref=leaving.at[part, :, pl.ds(size, size)],
            dst_ref=arriving.at[part, :, pl.ds(size, size)],
            send_sem=scatter_send.at[part, step],
            recv_sem=scatter_recv.at[part, step],
            device_id=partner(orders[part][step]),
            device_id_type=MESH,
        )

    def scatter_start(part, step):
        size = 2**step
        mine = lax.div(places[part], size)
        away = (mine + 1 - 2 * lax.rem(mine, 2)) * size
        leaving[part, :, size : 2 * size] = total[part, :, pl.ds(away, size)].astype(bf16)
        scatter_copy(part, step).start()

    def scatter_turn(part, step):
        size = 2**step
        scatter_copy(part, step).wait()
        keep = pl.ds(lax.div(places[part], size) * size, size)
        total[part, :, keep] = total[part, :, keep] + arriving[part, :, size : 2 * size].astype(f32)
        if step:
            scatter_start(part, step - 1)

    pair_bit = orders[0][-1]
    pair_half = bit_of(pair_bit)
    sum_orders = [orders[0][:-1], orders[0][:-1][::-1]]

    def pair_copy():
        return pltpu.make_async_remote_copy(
            src_ref=sums.at[pl.ds((1 - pair_half) * 2, 2)],
            dst_ref=sums_first,
            send_sem=sum_send.at[0],
            recv_sem=sum_recv.at[0],
            device_id=partner(pair_bit),
            device_id_type=MESH,
        )

    def run_copy(step, half):
        return pltpu.make_async_remote_copy(
            src_ref=sums_run.at[step, half],
            dst_ref=sums_in.at[step, half],
            send_sem=sum_send.at[1 + 2 * step + half],
            recv_sem=sum_recv.at[1 + 2 * step + half],
            device_id=partner(sum_orders[half][step]),
            device_id_type=MESH,
        )

    def share_copy():
        own = sums_all.at[pl.ds(pair_half * 2, 2)]
        return pltpu.make_async_remote_copy(
            src_ref=own,
            dst_ref=own,
            send_sem=sum_send.at[2 * steps - 1],
            recv_sem=sum_recv.at[2 * steps - 1],
            device_id=partner(pair_bit),
            device_id_type=MESH,
        )

    def sum_turn(step):
        last = steps - 1
        if step == 0:
            pair_copy().wait()
            sums_run[0] = sums[pl.ds(pair_half * 2, 2)] + sums_first[...]
        else:
            for half in range(2):
                run_copy(step - 1, half).wait()
                added = sums_run[step - 1, half] + sums_in[step - 1, half]
                if step < last:
                    sums_run[step, half] = added
                    run_copy(step, half).start()
                else:
                    sums_all[pl.ds(pair_half * 2 + half, 1)] = added[None]
            if step == last:
                share_copy().start()
            return
        for half in range(2):
            run_copy(0, half).start()

    def put_sum(at, lanes, value):
        sums[at // 16, at % 16 : at % 16 + 1, lanes] = value

    every = slice(0, channels)
    xpad[...] = jnp.zeros_like(xpad)
    center = xpad.at[pl.ds(3, height), pl.ds(EDGE, width)]
    moves = []
    for part in range(parts):
        for which, source in enumerate((win_hbm, wout_hbm)):
            moves.append(
                (source.at[pl.ds(part * unit_rows, unit_rows)], weights.at[part, which, places[part]])
            )
    moves += [
        (x_hbm, center),
        (cot_hbm, cot_ref),
        (scale_hbm, scale_ref),
        (taps_hbm, taps_ref),
        (bin_hbm, bin_ref),
        (gain_hbm, gain_ref),
        (offset_hbm, offset_ref),
        (bout_hbm, bout_ref),
    ]
    moves = [
        pltpu.make_async_copy(source, target, local_sem.at[at])
        for at, (source, target) in enumerate(moves)
    ]
    for move in moves:
        move.start()
    gpad[...] = jnp.zeros_like(gpad)

    barrier = pltpu.get_barrier_semaphore()
    expected = steps
    for b in range(steps):
        pl.semaphore_signal(barrier, inc=1, device_id=partner(b), device_id_type=MESH)
    for side in SIDES:
        here = exists(side)
        expected = expected + jnp.where(here, 1, 0)

        @pl.when(here)
        def _():
            pl.semaphore_signal(
                barrier, inc=1, device_id=(row + side[0], col + side[1]), device_id_type=MESH
            )

    pl.semaphore_wait(barrier, expected)

    halo_start(x_hbm, xpad, 0)
    for move in moves[: 2 * parts]:
        move.wait()
    for part in range(parts):
        gather_turn(part, 0)
    for move in moves[2 * parts :]:
        move.wait()

    def as_row(ref):
        return ref[...].reshape(1, ref.shape[0])

    gain, offset = as_row(gain_ref), as_row(offset_ref)
    out_bias, scale = as_row(bout_ref), as_row(scale_ref)
    sums[3] = jnp.zeros((16, channels), f32)
    grad_mixed = cot_ref[...].astype(f32).reshape(pixels, channels) * scale
    mixed_low[...] = grad_mixed.astype(bf16)
    put_sum(51, every, jnp.sum(grad_mixed, 0, keepdims=True))

    for part in range(parts):
        gather_turn(part, 1)

    owners = []
    for order in orders:
        owners.append(
            [
                sum(((place >> step) & 1) << b for step, b in enumerate(order))
                for place in range(2**steps)
            ]
        )
    bias_all = as_row(bin_ref)
    biases = []
    for part in range(parts):
        starts = [(owner * parts + part) * unit_rows for owner in owners[part]]
        biases.append(
            jnp.concatenate([bias_all[:, at : at + unit_rows] for at in starts], 1)
        )

    halo_wait(x_hbm, xpad, 0)
    wide[...] = xpad[:, 8 : width + 24].astype(f32)

    def window(shift, lanes):
        return wide[:, 5 + shift : 5 + shift + width, lanes]

    def stencil(lanes, flip):
        result = jnp.zeros((height, width, LANES), f32)
        for tap_col in range(7):
            shifted = window(tap_col, lanes)
            for tap_row in range(7):
                a, b = (6 - tap_row, 6 - tap_col) if flip else (tap_row, tap_col)
                result = result + shifted[tap_row : tap_row + height] * taps_ref[a, b : b + 1, lanes]
        return result

    blocks = channels // LANES
    for block in range(blocks):
        lanes = slice(block * LANES, (block + 1) * LANES)
        conv[:, lanes] = stencil(lanes, False).reshape(pixels, LANES)
        if block == 0:
            for part in range(parts):
                gather_turn(part, 2)

    def norm_tile(tile, carry):
        at = pl.ds(pl.multiple_of(tile * TILE, TILE), TILE)
        centered = conv[at, :]
        centered = centered - jnp.mean(centered, -1, keepdims=True)
        inv_std = lax.rsqrt(jnp.mean(centered * centered, -1, keepdims=True) + 1e-06)
        unit_scaled = centered * inv_std
        inv[at, :] = inv_std
        unit[at, :] = unit_scaled
        normed[at, :] = (unit_scaled * gain + offset).astype(bf16)
        return carry

    lax.fori_loop(0, pixels // TILE, norm_tile, 0)
    for step in range(3, steps):
        for part in range(parts):
            gather_turn(part, step)

    bias_sums = []
    for part in range(parts):
        gather_turn(part, steps)
        win = weights[part, 0].reshape(chunk, channels)
        wout = weights[part, 1].reshape(chunk, channels)
        hid[...] = lax.dot_general(normed[...], win, CONTRACT_LAST, preferred_element_type=f32)
        gact[...] = lax.dot_general(
            mixed_low[...], wout, CONTRACT_LAST, preferred_element_type=f32
        )

        def gelu_tile(tile, bias_sum):
            at = pl.ds(pl.multiple_of(tile * 16, 16), 16)
            act_value, slope = gelu_parts(hid[at, :] + biases[part])
            act[at, :] = act_value.astype(bf16)
            low = (gact[at, :] * slope).astype(bf16)
            ghid[at, :] = low
            return bias_sum + low.astype(f32)

        bias_sum = lax.fori_loop(
            0, pixels // 16, gelu_tile, jnp.zeros((16, chunk), f32)
        )
        bias_sums.append(jnp.sum(bias_sum, 0, keepdims=True))
        activated, grad_hidden = act[...], ghid[...]
        total[part, 1] = lax.dot_general(
            activated, mixed_low[...], CONTRACT_FIRST, preferred_element_type=f32
        ).reshape(-1, unit_rows, channels)
        total[part, 0] = lax.dot_general(
            grad_hidden, normed[...], CONTRACT_FIRST, preferred_element_type=f32
        ).reshape(-1, unit_rows, channels)
        scatter_start(part, steps - 1)
        mixed_term = jnp.dot(activated, wout, preferred_element_type=f32)
        gnorm_term = jnp.dot(grad_hidden, win, preferred_element_type=f32)
        mixed[...] = mixed_term if part == 0 else mixed[...] + mixed_term
        gnorm[...] = gnorm_term if part == 0 else gnorm[...] + gnorm_term
        if part:
            scatter_turn(part - 1, steps - 1)

    def back_tile(tile, carry):
        gain_sum, offset_sum = carry
        at = pl.ds(pl.multiple_of(tile * TILE, TILE), TILE)
        grad_normed = gnorm[at, :]
        unit_scaled = unit[at, :]
        product = grad_normed * unit_scaled
        scaled = grad_normed * gain
        grad_conv = inv[at, :] * (
            scaled
            - jnp.mean(scaled, -1, keepdims=True)
            - unit_scaled * jnp.mean(scaled * unit_scaled, -1, keepdims=True)
        )
        conv[at, :] = grad_conv
        normed[at, :] = grad_conv.astype(bf16)
        return (
            gain_sum + jnp.sum(product, 0, keepdims=True),
            offset_sum + jnp.sum(grad_normed, 0, keepdims=True),
        )

    none = jnp.zeros((1, channels), f32)
    gain_sum, offset_sum = lax.fori_loop(0, pixels // TILE, back_tile, (none, none))
    put_sum(49, every, gain_sum)
    put_sum(50, every, offset_sum)
    gpad[3 : 3 + height, EDGE : EDGE + width] = normed[...].reshape(height, width, channels)
    grad_block = gpad.at[pl.ds(3, height), pl.ds(EDGE, width)]
    halo_start(grad_block, gpad, 1)
    scatter_turn(2, steps - 1)

    mixed_full = mixed[...] + out_bias
    source = center[...].astype(f32).reshape(pixels, channels)
    out_ref[...] = (source + scale * mixed_full).astype(bf16).reshape(height, width, channels)
    grad_flow = cot_ref[...].astype(f32).reshape(pixels, channels)
    put_sum(52, every, jnp.sum(grad_flow * mixed_full, 0, keepdims=True))
    for line in range(4):
        pieces = []
        for owner in range(line * 2**steps // 4, (line + 1) * 2**steps // 4):
            for part in range(parts):
                at = owners[part].index(owner) * unit_rows
                pieces.append(bias_sums[part][:, at : at + unit_rows])
        put_sum(53 + line, every, jnp.concatenate(pieces, 1))

    for block in range(blocks):
        lanes = slice(block * LANES, (block + 1) * LANES)
        grad_part = conv[:, lanes].reshape(height, width, LANES)
        for tap_col in range(7):
            shifted = window(tap_col, lanes)
            for tap_row in range(7):
                at = tap_row * 7 + tap_col
                term = shifted[tap_row : tap_row + height] * grad_part
                put_sum(at, lanes, jnp.sum(term.reshape(pixels, LANES), 0, keepdims=True))
        if block < 2:
            scatter_turn(block, steps - 2)
    pair_copy().start()
    scatter_turn(2, steps - 2)
    scatter_turn(0, steps - 3)

    halo_wait(grad_block, gpad, 1)
    wide[...] = gpad[:, 8 : width + 24].astype(f32)
    for block in range(blocks):
        lanes = slice(block * LANES, (block + 1) * LANES)
        gin_ref[:, :, lanes] = (
            cot_ref[:, :, lanes].astype(f32) + stencil(lanes, True)
        ).astype(bf16)
        sum_turn(block)
        if block == 0:
            scatter_turn(1, steps - 3)
        elif block == 2:
            scatter_turn(2, steps - 3)
    pending = [(part, step) for step in range(steps - 4, -1, -1) for part in range(parts)]
    for step in range(blocks, steps):
        for turn in pending[:2]:
            scatter_turn(*turn)
        pending = pending[2:]
        sum_turn(step)
    for turn in pending:
        scatter_turn(*turn)
    for part in range(parts):
        at = slice(part * unit_rows, (part + 1) * unit_rows)
        own = total[part, :, pl.ds(places[part], 1)]
        gwin_ref[at, :] = own[0, 0]
        gwout_ref[at, :] = own[1, 0]
    share_copy().wait()
    everything = sums_all[...].reshape(64, channels)
    small_ref[...] = everything[0:53]
    for line in range(4):
        gbin_ref[line * channels : (line + 1) * channels] = everything[53 + line]


def write_out(*refs):
    count = len(refs) // 2
    sems = refs[-1]
    copies = [
        pltpu.make_async_copy(refs[at], refs[count + at], sems.at[at]) for at in range(count)
    ]
    for copy in copies:
        copy.start()
    for copy in copies:
        copy.wait()


def on_device(
    rows,
    cols,
    feature_map,
    kernel,
    ln_gain,
    ln_bias,
    w_in,
    b_in,
    w_out,
    b_out,
    layer_scale,
    cotangent,
):
    devices = rows * cols
    parts = 3
    height, width, channels = feature_map.shape
    units = w_out.shape[0]
    steps = devices.bit_length() - 1
    if units % (16 * parts) or devices != 2**steps or steps < 5 or devices * units != 4 * channels:
        return spread_plan(
            feature_map, kernel, ln_gain, ln_bias, w_in, b_in, w_out, b_out, layer_scale, cotangent
        )
    orders = bit_orders(rows, cols)
    piece = units // parts
    pixels = height * width
    f32, bf16 = jnp.float32, jnp.bfloat16
    padded_shape = (height + 6, width + 2 * EDGE, channels)
    outs = pl.pallas_call(
        functools.partial(fused_kernel, rows, cols, orders),
        out_shape=(
            jax.ShapeDtypeStruct(feature_map.shape, bf16),
            jax.ShapeDtypeStruct(feature_map.shape, bf16),
            jax.ShapeDtypeStruct((units, channels), f32),
            jax.ShapeDtypeStruct((units, channels), f32),
            jax.ShapeDtypeStruct((53, channels), f32),
            jax.ShapeDtypeStruct(b_in.shape, f32),
        ),
        in_specs=[pl.BlockSpec(memory_space=pltpu.HBM)] * 10,
        out_specs=(pl.BlockSpec(memory_space=pltpu.VMEM),) * 6,
        scratch_shapes=[
            pltpu.VMEM((pixels, devices * piece), f32),
            pltpu.VMEM((pixels, devices * piece), f32),
            pltpu.VMEM((pixels, devices * piece), bf16),
            pltpu.VMEM((pixels, devices * piece), bf16),
            pltpu.VMEM((pixels, 1), f32),
            pltpu.VMEM(cotangent.shape, bf16),
            pltpu.VMEM(kernel.shape, f32),
            pltpu.VMEM((channels,), f32),
            pltpu.VMEM((channels,), f32),
            pltpu.VMEM(b_in.shape, f32),
            pltpu.VMEM((channels,), f32),
            pltpu.VMEM((channels,), f32),
            pltpu.VMEM(padded_shape, bf16),
            pltpu.VMEM(padded_shape, bf16),
            pltpu.VMEM((height + 6, width + 16, channels), f32),
            pltpu.VMEM((pixels, channels), f32),
            pltpu.VMEM((pixels, channels), f32),
            pltpu.VMEM((pixels, channels), bf16),
            pltpu.VMEM((pixels, channels), bf16),
            pltpu.VMEM((pixels, channels), f32),
            pltpu.VMEM((pixels, channels), f32),
            pltpu.VMEM((parts, 2, devices, piece, channels), bf16),
            pltpu.VMEM((parts, 2, devices, piece, channels), f32),
            pltpu.VMEM((parts, 2, devices, piece, channels), bf16),
            pltpu.VMEM((parts, 2, devices, piece, channels), bf16),
            pltpu.VMEM((4, 16, channels), f32),
            pltpu.VMEM((2, 16, channels), f32),
            pltpu.VMEM((steps - 1, 2, 16, channels), f32),
            pltpu.VMEM((steps - 1, 2, 16, channels), f32),
            pltpu.VMEM((4, 16, channels), f32),
            pltpu.SemaphoreType.DMA((2 * parts + 8,)),
            pltpu.SemaphoreType.DMA((2, len(SIDES))),
            pltpu.SemaphoreType.DMA((2, len(SIDES))),
            pltpu.SemaphoreType.DMA((parts, steps)),
            pltpu.SemaphoreType.DMA((parts, steps)),
            pltpu.SemaphoreType.DMA((parts, steps)),
            pltpu.SemaphoreType.DMA((parts, steps)),
            pltpu.SemaphoreType.DMA((2 * steps,)),
            pltpu.SemaphoreType.DMA((2 * steps,)),
        ],
        compiler_params=pltpu.CompilerParams(
            collective_id=0, has_side_effects=True, vmem_limit_bytes=32 * 2**20
        ),
        name="convnext_block",
    )(
        feature_map,
        kernel,
        ln_gain,
        ln_bias,
        w_in.T,
        b_in,
        w_out,
        b_out,
        layer_scale,
        cotangent,
    )
    outs = pl.pallas_call(
        write_out,
        out_shape=tuple(jax.ShapeDtypeStruct(out.shape, out.dtype) for out in outs),
        in_specs=[pl.BlockSpec(memory_space=pltpu.VMEM)] * 6,
        out_specs=(pl.BlockSpec(memory_space=pltpu.HBM),) * 6,
        scratch_shapes=[pltpu.SemaphoreType.DMA((6,))],
        compiler_params=pltpu.CompilerParams(vmem_limit_bytes=4 * 2**20),
        name="write_out",
    )(*outs)
    block_out, grad_input, grad_win, grad_wout, small_grads, grad_b_in = outs
    return (block_out, grad_input, grad_win.T, grad_wout, small_grads, grad_b_in)


def solution(mesh):
    placed = (
        P("row", "col", None),
        P(),
        P(),
        P(),
        P(None, ("row", "col")),
        P(),
        P(("row", "col"), None),
        P(),
        P(),
        P("row", "col", None),
    )
    return jax.shard_map(
        functools.partial(on_device, mesh.shape["row"], mesh.shape["col"]),
        mesh=mesh,
        in_specs=placed,
        out_specs=(
            P("row", "col", None),
            P("row", "col", None),
            P(None, ("row", "col")),
            P(("row", "col"), None),
            P(),
            P(),
        ),
        check_vma=False,
    )
```

```python
import functools
import math

import jax
import jax.numpy as jnp
from jax import lax
from jax.experimental import pallas as pl
from jax.experimental.pallas import tpu as pltpu
from jax.sharding import PartitionSpec as P


def padded_2(x, sides, width):
    for axis, dim in sides:
        peers, length = (lax.axis_size(axis), x.shape[dim])
        up = [(i, (i + 1) % peers) for i in range(peers - 1)]
        down = [(j, i) for i, j in up]
        last = lax.slice_in_dim(x, length - width, length, axis=dim)
        first = lax.slice_in_dim(x, 0, width, axis=dim)
        before = lax.ppermute(last, axis, up)
        after = lax.ppermute(first, axis, down)
        x = jnp.concatenate([before, x, after], axis=dim)
    return x


def gelu_parts(hidden):
    normal_cdf = 0.5 * (1.0 + jax.scipy.special.erf(hidden * (1.0 / math.sqrt(2.0))))
    density = jnp.exp(-0.5 * hidden * hidden) * (1.0 / math.sqrt(2.0 * math.pi))
    return (hidden * normal_cdf, normal_cdf + hidden * density)


def extend(field):
    return padded_2(field, (("row", 0), ("col", 1)), 3)


def spread_plan(
    feature_map, kernel, ln_gain, ln_bias, w_in, b_in, w_out, b_out, layer_scale, cotangent
):
    row_count, col_count, channels = feature_map.shape
    pixels = row_count * col_count
    padded = extend(feature_map).astype(jnp.float32)
    conv = jnp.zeros((row_count, col_count, channels), jnp.float32)
    for tap_row in range(7):
        for tap_col in range(7):
            conv = (
                conv
                + padded[tap_row : tap_row + row_count, tap_col : tap_col + col_count]
                * kernel[tap_row, tap_col]
            )
    average = jnp.mean(conv, -1, keepdims=True)
    centered = conv - average
    variance = jnp.mean(centered * centered, -1, keepdims=True)
    inv_std = lax.rsqrt(variance + 1e-06)
    unit_scaled = centered * inv_std
    normed = (unit_scaled * ln_gain + ln_bias).astype(jnp.bfloat16).reshape(pixels, channels)
    contract_last = (((1,), (1,)), ((), ()))
    contract_first = (((0,), (0,)), ((), ()))
    w_in_full = lax.all_gather(w_in, ("row", "col"), axis=1, tiled=True)
    w_out_full = lax.all_gather(w_out, ("row", "col"), axis=0, tiled=True)
    hidden = jnp.dot(normed, w_in_full, preferred_element_type=jnp.float32) + b_in
    act_value, slope = gelu_parts(hidden)
    activated = act_value.astype(jnp.bfloat16)
    mixed = jnp.dot(activated, w_out_full, preferred_element_type=jnp.float32) + b_out
    source = feature_map.astype(jnp.float32).reshape(pixels, channels)
    block_out = (
        (source + layer_scale * mixed).astype(jnp.bfloat16).reshape(row_count, col_count, channels)
    )
    grad_flow = cotangent.astype(jnp.float32).reshape(pixels, channels)
    grad_mixed = grad_flow * layer_scale
    mixed_low = grad_mixed.astype(jnp.bfloat16)
    grad_act = lax.dot_general(
        mixed_low, w_out_full, contract_last, preferred_element_type=jnp.float32
    )
    grad_hidden = (grad_act * slope).astype(jnp.bfloat16)
    grad_w_out = lax.psum_scatter(
        lax.dot_general(activated, mixed_low, contract_first, preferred_element_type=jnp.float32),
        ("row", "col"),
        scatter_dimension=0,
        tiled=True,
    )
    win_term = lax.dot_general(
        normed, grad_hidden, contract_first, preferred_element_type=jnp.float32
    )
    grad_w_in = lax.psum_scatter(win_term, ("row", "col"), scatter_dimension=1, tiled=True)
    grad_normed = lax.dot_general(
        grad_hidden, w_in_full, contract_last, preferred_element_type=jnp.float32
    )
    grad_normed = grad_normed.reshape(row_count, col_count, channels)
    grad_gain = jnp.sum(grad_normed * unit_scaled, (0, 1))
    grad_lnb = jnp.sum(grad_normed, (0, 1))
    scaled_grad = grad_normed * ln_gain
    grad_conv = inv_std * (
        scaled_grad
        - jnp.mean(scaled_grad, -1, keepdims=True)
        - unit_scaled * jnp.mean(scaled_grad * unit_scaled, -1, keepdims=True)
    )
    tap_terms = []
    for tap_row in range(7):
        for tap_col in range(7):
            tap_terms.append(
                jnp.sum(
                    padded[tap_row : tap_row + row_count, tap_col : tap_col + col_count]
                    * grad_conv,
                    (0, 1),
                )
            )
    grad_pad = extend(grad_conv.astype(jnp.bfloat16)).astype(jnp.float32)
    back_conv = jnp.zeros((row_count, col_count, channels), jnp.float32)
    for tap_row in range(7):
        for tap_col in range(7):
            back_conv = (
                back_conv
                + grad_pad[
                    6 - tap_row : 6 - tap_row + row_count, 6 - tap_col : 6 - tap_col + col_count
                ]
                * kernel[tap_row, tap_col]
            )
    grad_input = (cotangent.astype(jnp.float32) + back_conv).astype(jnp.bfloat16)
    small_local = jnp.concatenate(
        [
            jnp.stack(tap_terms, 0),
            grad_gain[None],
            grad_lnb[None],
            jnp.sum(grad_mixed, 0)[None],
            jnp.sum(grad_flow * mixed, 0)[None],
        ],
        0,
    )
    bias_local = jnp.sum(grad_hidden.astype(jnp.float32), 0)
    small_grads, grad_b_in = lax.psum((small_local, bias_local), ("row", "col"))
    return (block_out, grad_input, grad_w_in, grad_w_out, small_grads, grad_b_in)


MESH = pl.DeviceIdType.MESH
SIDES = [(a, b) for a in (-1, 0, 1) for b in (-1, 0, 1) if (a, b) != (0, 0)]
EDGE = 16
TILE = 32
LANES = 128
CONTRACT_LAST = (((1,), (1,)), ((), ()))
CONTRACT_FIRST = (((0,), (0,)), ((), ()))


def bit_orders(rows, cols):
    bits = (rows * cols).bit_length() - 1
    pair = cols.bit_length() - 1
    rest = [b for b in range(bits - 1, -1, -1) if b != pair]
    orders = [rest[-2:] + rest[:-2], rest[-1:] + rest[:-1], rest]
    return [order + [pair] for order in orders]


def fused_kernel(
    rows,
    cols,
    orders,
    x_hbm,
    taps_hbm,
    gain_hbm,
    offset_hbm,
    win_hbm,
    bin_hbm,
    wout_hbm,
    bout_hbm,
    scale_hbm,
    cot_hbm,
    out_ref,
    gin_ref,
    gwin_ref,
    gwout_ref,
    small_ref,
    gbin_ref,
    hid,
    gact,
    act,
    ghid,
    inv,
    cot_ref,
    taps_ref,
    gain_ref,
    offset_ref,
    bin_ref,
    bout_ref,
    scale_ref,
    xpad,
    gpad,
    wide,
    conv,
    unit,
    normed,
    mixed_low,
    mixed,
    gnorm,
    weights,
    total,
    leaving,
    arriving,
    sums,
    sums_first,
    sums_run,
    sums_in,
    sums_all,
    local_sem,
    halo_send,
    halo_recv,
    gather_send,
    gather_recv,
    scatter_send,
    scatter_recv,
    sum_send,
    sum_recv,
):
    height, width, channels = cot_ref.shape
    pixels = height * width
    parts = len(orders)
    steps = len(orders[0])
    unit_rows = weights.shape[3]
    chunk = weights.shape[2] * unit_rows
    row, col = lax.axis_index("row"), lax.axis_index("col")
    me = row * cols + col
    f32, bf16 = jnp.float32, jnp.bfloat16

    def bit_of(b):
        return lax.rem(lax.div(me, 2**b), 2)

    def partner(b):
        other = me + (1 - 2 * bit_of(b)) * 2**b
        return (lax.div(other, cols), lax.rem(other, cols))

    places = []
    for order in orders:
        place = 0
        for step, b in enumerate(order):
            place = place + bit_of(b) * 2**step
        places.append(place)

    def exists(side):
        dr, dc = side
        there = None
        for delta, at, count in ((dr, row, rows), (dc, col, cols)):
            if delta:
                ok = at > 0 if delta < 0 else at < count - 1
                there = ok if there is None else jnp.logical_and(there, ok)
        return there

    def halo_copy(source, pad, which, side, receiving):
        dr, dc = side
        at = SIDES.index(side)
        back = SIDES.index((-dr, -dc))
        row_from = {-1: pl.ds(0, 3), 0: pl.ds(0, height), 1: pl.ds(height - 3, 3)}[dr]
        col_from = {-1: pl.ds(0, EDGE), 0: pl.ds(0, width), 1: pl.ds(width - EDGE, EDGE)}[dc]
        into_r, into_c = (dr, dc) if receiving else (-dr, -dc)
        row_to = {-1: pl.ds(0, 3), 0: pl.ds(3, height), 1: pl.ds(height + 3, 3)}[into_r]
        col_to = {-1: pl.ds(0, EDGE), 0: pl.ds(EDGE, width), 1: pl.ds(width + EDGE, EDGE)}[into_c]
        return pltpu.make_async_remote_copy(
            src_ref=source.at[row_from, col_from],
            dst_ref=pad.at[row_to, col_to],
            send_sem=halo_send.at[which, at],
            recv_sem=halo_recv.at[which, back if receiving else at],
            device_id=(row + dr, col + dc),
            device_id_type=MESH,
        )

    def halo_start(source, pad, which):
        for side in SIDES:

            @pl.when(exists(side))
            def _():
                halo_copy(source, pad, which, side, False).start()

    def halo_wait(source, pad, which):
        for side in SIDES:

            @pl.when(exists(side))
            def _():
                halo_copy(source, pad, which, side, False).wait_send()
                halo_copy(source, pad, which, side, True).wait_recv()

    def gather_copy(part, step):
        size = 2**step
        held = weights.at[part, :, pl.ds(lax.div(places[part], size) * size, size)]
        return pltpu.make_async_remote_copy(
            src_ref=held,
            dst_ref=held,
            send_sem=gather_send.at[part, step],
            recv_sem=gather_recv.at[part, step],
            device_id=partner(orders[part][step]),
            device_id_type=MESH,
        )

    def gather_turn(part, step):
        if step:
            gather_copy(part, step - 1).wait()
        if step < steps:
            gather_copy(part, step).start()

    def scatter_copy(part, step):
        size = 2**step
        return pltpu.make_async_remote_copy(
            src_ref=leaving.at[part, :, pl.ds(size, size)],
            dst_ref=arriving.at[part, :, pl.ds(size, size)],
            send_sem=scatter_send.at[part, step],
            recv_sem=scatter_recv.at[part, step],
            device_id=partner(orders[part][step]),
            device_id_type=MESH,
        )

    def scatter_start(part, step):
        size = 2**step
        mine = lax.div(places[part], size)
        away = (mine + 1 - 2 * lax.rem(mine, 2)) * size
        leaving[part, :, size : 2 * size] = total[part, :, pl.ds(away, size)].astype(bf16)
        scatter_copy(part, step).start()

    def scatter_turn(part, step):
        size = 2**step
        scatter_copy(part, step).wait()
        keep = pl.ds(lax.div(places[part], size) * size, size)
        total[part, :, keep] = total[part, :, keep] + arriving[part, :, size : 2 * size].astype(f32)
        if step:
            scatter_start(part, step - 1)

    pair_bit = orders[0][-1]
    pair_half = bit_of(pair_bit)
    sum_orders = [orders[0][:-1], orders[0][:-1][::-1]]

    def pair_copy():
        return pltpu.make_async_remote_copy(
            src_ref=sums.at[pl.ds((1 - pair_half) * 2, 2)],
            dst_ref=sums_first,
            send_sem=sum_send.at[0],
            recv_sem=sum_recv.at[0],
            device_id=partner(pair_bit),
            device_id_type=MESH,
        )

    def run_copy(step, half):
        return pltpu.make_async_remote_copy(
            src_ref=sums_run.at[step, half],
            dst_ref=sums_in.at[step, half],
            send_sem=sum_send.at[1 + 2 * step + half],
            recv_sem=sum_recv.at[1 + 2 * step + half],
            device_id=partner(sum_orders[half][step]),
            device_id_type=MESH,
        )

    def share_copy():
        own = sums_all.at[pl.ds(pair_half * 2, 2)]
        return pltpu.make_async_remote_copy(
            src_ref=own,
            dst_ref=own,
            send_sem=sum_send.at[2 * steps - 1],
            recv_sem=sum_recv.at[2 * steps - 1],
            device_id=partner(pair_bit),
            device_id_type=MESH,
        )

    def sum_turn(step):
        last = steps - 1
        if step == 0:
            pair_copy().wait()
            sums_run[0] = sums[pl.ds(pair_half * 2, 2)] + sums_first[...]
        else:
            for half in range(2):
                run_copy(step - 1, half).wait()
                added = sums_run[step - 1, half] + sums_in[step - 1, half]
                if step < last:
                    sums_run[step, half] = added
                    run_copy(step, half).start()
                else:
                    sums_all[pl.ds(pair_half * 2 + half, 1)] = added[None]
            if step == last:
                share_copy().start()
            return
        for half in range(2):
            run_copy(0, half).start()

    def put_sum(at, lanes, value):
        sums[at // 16, at % 16 : at % 16 + 1, lanes] = value

    every = slice(0, channels)
    xpad[...] = jnp.zeros_like(xpad)
    center = xpad.at[pl.ds(3, height), pl.ds(EDGE, width)]
    moves = []
    for part in range(parts):
        for which, source in enumerate((win_hbm, wout_hbm)):
            moves.append(
                (source.at[pl.ds(part * unit_rows, unit_rows)], weights.at[part, which, places[part]])
            )
    moves += [
        (x_hbm, center),
        (cot_hbm, cot_ref),
        (scale_hbm, scale_ref),
        (taps_hbm, taps_ref),
        (bin_hbm, bin_ref),
        (gain_hbm, gain_ref),
        (offset_hbm, offset_ref),
        (bout_hbm, bout_ref),
    ]
    moves = [
        pltpu.make_async_copy(source, target, local_sem.at[at])
        for at, (source, target) in enumerate(moves)
    ]
    for move in moves:
        move.start()
    gpad[...] = jnp.zeros_like(gpad)

    barrier = pltpu.get_barrier_semaphore()
    expected = steps
    for b in range(steps):
        pl.semaphore_signal(barrier, inc=1, device_id=partner(b), device_id_type=MESH)
    for side in SIDES:
        here = exists(side)
        expected = expected + jnp.where(here, 1, 0)

        @pl.when(here)
        def _():
            pl.semaphore_signal(
                barrier, inc=1, device_id=(row + side[0], col + side[1]), device_id_type=MESH
            )

    pl.semaphore_wait(barrier, expected)

    halo_start(x_hbm, xpad, 0)
    for move in moves[: 2 * parts]:
        move.wait()
    for part in range(parts):
        gather_turn(part, 0)
    for move in moves[2 * parts :]:
        move.wait()

    def as_row(ref):
        return ref[...].reshape(1, ref.shape[0])

    gain, offset = as_row(gain_ref), as_row(offset_ref)
    out_bias, scale = as_row(bout_ref), as_row(scale_ref)
    sums[3] = jnp.zeros((16, channels), f32)
    grad_mixed = cot_ref[...].astype(f32).reshape(pixels, channels) * scale
    mixed_low[...] = grad_mixed.astype(bf16)
    put_sum(51, every, jnp.sum(grad_mixed, 0, keepdims=True))

    for part in range(parts):
        gather_turn(part, 1)

    owners = []
    for order in orders:
        owners.append(
            [
                sum(((place >> step) & 1) << b for step, b in enumerate(order))
                for place in range(2**steps)
            ]
        )
    bias_all = as_row(bin_ref)
    biases = []
    for part in range(parts):
        starts = [(owner * parts + part) * unit_rows for owner in owners[part]]
        biases.append(
            jnp.concatenate([bias_all[:, at : at + unit_rows] for at in starts], 1)
        )

    halo_wait(x_hbm, xpad, 0)
    wide[...] = xpad[:, 8 : width + 24].astype(f32)

    def window(shift, lanes):
        return wide[:, 5 + shift : 5 + shift + width, lanes]

    def stencil(lanes, flip):
        result = jnp.zeros((height, width, LANES), f32)
        for tap_col in range(7):
            shifted = window(tap_col, lanes)
            for tap_row in range(7):
                a, b = (6 - tap_row, 6 - tap_col) if flip else (tap_row, tap_col)
                result = result + shifted[tap_row : tap_row + height] * taps_ref[a, b : b + 1, lanes]
        return result

    blocks = channels // LANES
    for block in range(blocks):
        lanes = slice(block * LANES, (block + 1) * LANES)
        conv[:, lanes] = stencil(lanes, False).reshape(pixels, LANES)
        if block == 0:
            for part in range(parts):
                gather_turn(part, 2)

    def norm_tile(tile, carry):
        at = pl.ds(pl.multiple_of(tile * TILE, TILE), TILE)
        centered = conv[at, :]
        centered = centered - jnp.mean(centered, -1, keepdims=True)
        inv_std = lax.rsqrt(jnp.mean(centered * centered, -1, keepdims=True) + 1e-06)
        unit_scaled = centered * inv_std
        inv[at, :] = inv_std
        unit[at, :] = unit_scaled
        normed[at, :] = (unit_scaled * gain + offset).astype(bf16)
        return carry

    lax.fori_loop(0, pixels // TILE, norm_tile, 0)
    for step in range(3, steps):
        for part in range(parts):
            gather_turn(part, step)

    bias_sums = []
    for part in range(parts):
        gather_turn(part, steps)
        win = weights[part, 0].reshape(chunk, channels)
        wout = weights[part, 1].reshape(chunk, channels)
        hid[...] = lax.dot_general(normed[...], win, CONTRACT_LAST, preferred_element_type=f32)
        gact[...] = lax.dot_general(
            mixed_low[...], wout, CONTRACT_LAST, preferred_element_type=f32
        )

        def gelu_tile(tile, bias_sum):
            at = pl.ds(pl.multiple_of(tile * 16, 16), 16)
            act_value, slope = gelu_parts(hid[at, :] + biases[part])
            act[at, :] = act_value.astype(bf16)
            low = (gact[at, :] * slope).astype(bf16)
            ghid[at, :] = low
            return bias_sum + low.astype(f32)

        bias_sum = lax.fori_loop(
            0, pixels // 16, gelu_tile, jnp.zeros((16, chunk), f32)
        )
        bias_sums.append(jnp.sum(bias_sum, 0, keepdims=True))
        activated, grad_hidden = act[...], ghid[...]
        total[part, 1] = lax.dot_general(
            activated, mixed_low[...], CONTRACT_FIRST, preferred_element_type=f32
        ).reshape(-1, unit_rows, channels)
        total[part, 0] = lax.dot_general(
            grad_hidden, normed[...], CONTRACT_FIRST, preferred_element_type=f32
        ).reshape(-1, unit_rows, channels)
        scatter_start(part, steps - 1)
        mixed_term = jnp.dot(activated, wout, preferred_element_type=f32)
        gnorm_term = jnp.dot(grad_hidden, win, preferred_element_type=f32)
        mixed[...] = mixed_term if part == 0 else mixed[...] + mixed_term
        gnorm[...] = gnorm_term if part == 0 else gnorm[...] + gnorm_term
        if part:
            scatter_turn(part - 1, steps - 1)

    def back_tile(tile, carry):
        gain_sum, offset_sum = carry
        at = pl.ds(pl.multiple_of(tile * TILE, TILE), TILE)
        grad_normed = gnorm[at, :]
        unit_scaled = unit[at, :]
        product = grad_normed * unit_scaled
        scaled = grad_normed * gain
        grad_conv = inv[at, :] * (
            scaled
            - jnp.mean(scaled, -1, keepdims=True)
            - unit_scaled * jnp.mean(scaled * unit_scaled, -1, keepdims=True)
        )
        conv[at, :] = grad_conv
        normed[at, :] = grad_conv.astype(bf16)
        return (
            gain_sum + jnp.sum(product, 0, keepdims=True),
            offset_sum + jnp.sum(grad_normed, 0, keepdims=True),
        )

    none = jnp.zeros((1, channels), f32)
    gain_sum, offset_sum = lax.fori_loop(0, pixels // TILE, back_tile, (none, none))
    put_sum(49, every, gain_sum)
    put_sum(50, every, offset_sum)
    gpad[3 : 3 + height, EDGE : EDGE + width] = normed[...].reshape(height, width, channels)
    grad_block = gpad.at[pl.ds(3, height), pl.ds(EDGE, width)]
    halo_start(grad_block, gpad, 1)
    scatter_turn(2, steps - 1)

    mixed_full = mixed[...] + out_bias
    source = center[...].astype(f32).reshape(pixels, channels)
    out_ref[...] = (source + scale * mixed_full).astype(bf16).reshape(height, width, channels)
    grad_flow = cot_ref[...].astype(f32).reshape(pixels, channels)
    put_sum(52, every, jnp.sum(grad_flow * mixed_full, 0, keepdims=True))
    for line in range(4):
        pieces = []
        for owner in range(line * 2**steps // 4, (line + 1) * 2**steps // 4):
            for part in range(parts):
                at = owners[part].index(owner) * unit_rows
                pieces.append(bias_sums[part][:, at : at + unit_rows])
        put_sum(53 + line, every, jnp.concatenate(pieces, 1))

    for block in range(blocks):
        lanes = slice(block * LANES, (block + 1) * LANES)
        grad_part = conv[:, lanes].reshape(height, width, LANES)
        for tap_col in range(7):
            shifted = window(tap_col, lanes)
            for tap_row in range(7):
                at = tap_row * 7 + tap_col
                term = shifted[tap_row : tap_row + height] * grad_part
                put_sum(at, lanes, jnp.sum(term.reshape(pixels, LANES), 0, keepdims=True))
        if block < 2:
            scatter_turn(block, steps - 2)
    pair_copy().start()
    scatter_turn(2, steps - 2)
    scatter_turn(0, steps - 3)

    halo_wait(grad_block, gpad, 1)
    wide[...] = gpad[:, 8 : width + 24].astype(f32)
    for block in range(blocks):
        lanes = slice(block * LANES, (block + 1) * LANES)
        gin_ref[:, :, lanes] = (
            cot_ref[:, :, lanes].astype(f32) + stencil(lanes, True)
        ).astype(bf16)
        sum_turn(block)
        if block == 0:
            scatter_turn(1, steps - 3)
        elif block == 2:
            scatter_turn(2, steps - 3)
    pending = [(part, step) for step in range(steps - 4, -1, -1) for part in range(parts)]
    for step in range(blocks, steps):
        for turn in pending[:2]:
            scatter_turn(*turn)
        pending = pending[2:]
        sum_turn(step)
    for turn in pending:
        scatter_turn(*turn)
    for part in range(parts):
        at = slice(part * unit_rows, (part + 1) * unit_rows)
        own = total[part, :, pl.ds(places[part], 1)]
        gwin_ref[at, :] = own[0, 0]
        gwout_ref[at, :] = own[1, 0]
    share_copy().wait()
    everything = sums_all[...].reshape(64, channels)
    small_ref[...] = everything[0:53]
    for line in range(4):
        gbin_ref[line * channels : (line + 1) * channels] = everything[53 + line]


def write_out(*refs):
    count = len(refs) // 2
    sems = refs[-1]
    copies = [
        pltpu.make_async_copy(refs[at], refs[count + at], sems.at[at]) for at in range(count)
    ]
    for copy in copies:
        copy.start()
    for copy in copies:
        copy.wait()


def on_device(
    rows,
    cols,
    feature_map,
    kernel,
    ln_gain,
    ln_bias,
    w_in,
    b_in,
    w_out,
    b_out,
    layer_scale,
    cotangent,
):
    devices = rows * cols
    parts = 3
    height, width, channels = feature_map.shape
    units = w_out.shape[0]
    steps = devices.bit_length() - 1
    if units % (16 * parts) or devices != 2**steps or steps < 5 or devices * units != 4 * channels:
        return spread_plan(
            feature_map, kernel, ln_gain, ln_bias, w_in, b_in, w_out, b_out, layer_scale, cotangent
        )
    orders = bit_orders(rows, cols)
    piece = units // parts
    pixels = height * width
    f32, bf16 = jnp.float32, jnp.bfloat16
    padded_shape = (height + 6, width + 2 * EDGE, channels)
    outs = pl.pallas_call(
        functools.partial(fused_kernel, rows, cols, orders),
        out_shape=(
            jax.ShapeDtypeStruct(feature_map.shape, bf16),
            jax.ShapeDtypeStruct(feature_map.shape, bf16),
            jax.ShapeDtypeStruct((units, channels), f32),
            jax.ShapeDtypeStruct((units, channels), f32),
            jax.ShapeDtypeStruct((53, channels), f32),
            jax.ShapeDtypeStruct(b_in.shape, f32),
        ),
        in_specs=[pl.BlockSpec(memory_space=pltpu.HBM)] * 10,
        out_specs=(pl.BlockSpec(memory_space=pltpu.VMEM),) * 6,
        scratch_shapes=[
            pltpu.VMEM((pixels, devices * piece), f32),
            pltpu.VMEM((pixels, devices * piece), f32),
            pltpu.VMEM((pixels, devices * piece), bf16),
            pltpu.VMEM((pixels, devices * piece), bf16),
            pltpu.VMEM((pixels, 1), f32),
            pltpu.VMEM(cotangent.shape, bf16),
            pltpu.VMEM(kernel.shape, f32),
            pltpu.VMEM((channels,), f32),
            pltpu.VMEM((channels,), f32),
            pltpu.VMEM(b_in.shape, f32),
            pltpu.VMEM((channels,), f32),
            pltpu.VMEM((channels,), f32),
            pltpu.VMEM(padded_shape, bf16),
            pltpu.VMEM(padded_shape, bf16),
            pltpu.VMEM((height + 6, width + 16, channels), f32),
            pltpu.VMEM((pixels, channels), f32),
            pltpu.VMEM((pixels, channels), f32),
            pltpu.VMEM((pixels, channels), bf16),
            pltpu.VMEM((pixels, channels), bf16),
            pltpu.VMEM((pixels, channels), f32),
            pltpu.VMEM((pixels, channels), f32),
            pltpu.VMEM((parts, 2, devices, piece, channels), bf16),
            pltpu.VMEM((parts, 2, devices, piece, channels), f32),
            pltpu.VMEM((parts, 2, devices, piece, channels), bf16),
            pltpu.VMEM((parts, 2, devices, piece, channels), bf16),
            pltpu.VMEM((4, 16, channels), f32),
            pltpu.VMEM((2, 16, channels), f32),
            pltpu.VMEM((steps - 1, 2, 16, channels), f32),
            pltpu.VMEM((steps - 1, 2, 16, channels), f32),
            pltpu.VMEM((4, 16, channels), f32),
            pltpu.SemaphoreType.DMA((2 * parts + 8,)),
            pltpu.SemaphoreType.DMA((2, len(SIDES))),
            pltpu.SemaphoreType.DMA((2, len(SIDES))),
            pltpu.SemaphoreType.DMA((parts, steps)),
            pltpu.SemaphoreType.DMA((parts, steps)),
            pltpu.SemaphoreType.DMA((parts, steps)),
            pltpu.SemaphoreType.DMA((parts, steps)),
            pltpu.SemaphoreType.DMA((2 * steps,)),
            pltpu.SemaphoreType.DMA((2 * steps,)),
        ],
        compiler_params=pltpu.CompilerParams(
            collective_id=0, has_side_effects=True, vmem_limit_bytes=60 * 2**20
        ),
        name="convnext_block",
    )(
        feature_map,
        kernel,
        ln_gain,
        ln_bias,
        w_in.T,
        b_in,
        w_out,
        b_out,
        layer_scale,
        cotangent,
    )
    outs = pl.pallas_call(
        write_out,
        out_shape=tuple(jax.ShapeDtypeStruct(out.shape, out.dtype) for out in outs),
        in_specs=[pl.BlockSpec(memory_space=pltpu.VMEM)] * 6,
        out_specs=(pl.BlockSpec(memory_space=pltpu.HBM),) * 6,
        scratch_shapes=[pltpu.SemaphoreType.DMA((6,))],
        compiler_params=pltpu.CompilerParams(vmem_limit_bytes=60 * 2**20),
        name="write_out",
    )(*outs)
    block_out, grad_input, grad_win, grad_wout, small_grads, grad_b_in = outs
    return (block_out, grad_input, grad_win.T, grad_wout, small_grads, grad_b_in)


def solution(mesh):
    placed = (
        P("row", "col", None),
        P(),
        P(),
        P(),
        P(None, ("row", "col")),
        P(),
        P(("row", "col"), None),
        P(),
        P(),
        P("row", "col", None),
    )
    return jax.shard_map(
        functools.partial(on_device, mesh.shape["row"], mesh.shape["col"]),
        mesh=mesh,
        in_specs=placed,
        out_specs=(
            P("row", "col", None),
            P("row", "col", None),
            P(None, ("row", "col")),
            P(("row", "col"), None),
            P(),
            P(),
        ),
        check_vma=False,
    )
```
